512 devices in a mesh: led: 8 (over z_hi, core), row: 64 (over y, x, z_lo).
Axes of the slice: x: 4, y: 8, z: 8 (z_hi: 4, z_lo: 2; z = z_hi * 2 + z_lo), core: 2. Of those that a mesh axis runs over, the one named last changes fastest.
Arguments:
- fields: float32 [2, 16, 2, 1024, 1024], P(None, 'led', None, 'row'), may hold values from -6 to 6
- phases: float32 [2, 1024, 1024], P(None, 'row'), may hold values from -3.140625 to 3.140625
- residual: float32 [16, 2, 1024, 1024], P('led', None, 'row'), may hold values from -6 to 6
- led_index: int32 [16], P('led'), may hold values from 0 to 224
Outputs:
- slopes: float32 [2, 1024, 1024], P(None, 'row', 'led')
- adjoint_wave: float32 [16, 2, 1024, 1024], P('led', None, 'row')
The draws below stay inside these ranges and needn't reach their ends.
All inputs are finite; a program needn't handle non-finite values.
Results may differ from the reference program's by a relative error of at most 0.0003.
Values sent between devices are 32-bit elements; how exact they have to be, the bound alone decides.
A program may use at most 64 MiB of HBM per device.

```python
import math
import jax
import jax.numpy as jnp
from jax import lax

N = 1024
SLICES = 2
GRID = 15
DZ = 64
SHIFT = 10
LEDS = 16


def draw_residual(key, part):
    key = jax.random.fold_in(key, 7)
    values = jnp.clip(jax.random.normal(key, (LEDS, 2, N, N), jnp.float32), -6.0, 6.0)
    return values


def with_ends(entries, own_key, low, high):
    spot = [jax.random.randint(jax.random.fold_in(own_key, axis), (), 0, length) for axis, length in enumerate(entries.shape)]
    main_axis = entries.shape.index(max(entries.shape))
    neighbour = spot[:main_axis] + [(spot[main_axis] + 1) % entries.shape[main_axis]] + spot[main_axis + 1:]
    return entries.at[tuple(spot)].set(low).at[tuple(neighbour)].set(high)


def level_of(key, dims, shards, least, top_value):
    def one(position, parts):
        draws = jax.random.uniform(jax.random.fold_in(jax.random.fold_in(key, 6), position), (parts,), jnp.float32, least / len(shards), top_value / len(shards))
        return jnp.repeat(jnp.exp(draws), dims[position] // parts).reshape((-1,) + (1,) * (len(dims) - position - 1))

    gain = one(*shards[0])
    for cut in shards[1:]:
        gain = gain * one(*cut)
    return gain


def bell_draw(own_key, extent, width, bound, cuts=(), dtype=jnp.bfloat16):
    drawn = jax.random.normal(own_key, extent, jnp.float32) * width
    if len(cuts) > 0:
        drawn = level_of(own_key, extent, cuts, -0.22, 0.18) * drawn
    return jnp.clip(drawn, min=-bound, max=bound).astype(dtype)


def setup_inputs(seed: int = 0) -> dict:
    arg_keys = jax.random.split(jax.random.key(seed), 5)
    return {
        "fields": bell_draw(arg_keys[0], (SLICES, LEDS, 2, N, N), 1.0, 6.0, ((1, 8), (3, 64)), jnp.float32),
        "phases": jnp.clip(jax.random.uniform(arg_keys[1], (SLICES, N, N), jnp.float32, -3.140625, 3.140625), -3.140625, 3.140625),
        "residual": draw_residual(jax.random.fold_in(arg_keys[4], 71), 0),
        "led_index": with_ends(jax.random.randint(arg_keys[3], (LEDS,), 0, GRID * GRID), jax.random.fold_in(arg_keys[3], 1), 0, (GRID * GRID) - 1).astype(jnp.int32),
    }


def wrapped(index, length):
    return (index + length // 2) % length - length // 2

def propagation_phase(led_index, freq_x, freq_y):
    shift_x = (led_index // GRID - GRID // 2) * SHIFT
    shift_y = (led_index % GRID - GRID // 2) * SHIFT
    along_x = (freq_x[None, :, None] + shift_x[:, None, None]).astype(jnp.float32) / N
    along_y = (freq_y[None, None, :] + shift_y[:, None, None]).astype(jnp.float32) / N
    return 2.0 * math.pi * DZ * (jnp.sqrt(1.0 - along_x * along_x - along_y * along_y) - 1.0)

def reference(fields, phases, residual, led_index):
    frequency = wrapped(jnp.arange(N).astype(jnp.int32), N)
    phase_angle = jnp.swapaxes(propagation_phase(led_index, frequency, frequency), 1, 2)
    kernel_conj = jnp.cos(phase_angle) - 1j * jnp.sin(phase_angle)
    wave = residual[:, 0] + 1j * residual[:, 1]
    slope_list = []
    for layer in reversed(range(SLICES)):
        spread = jnp.fft.ifft2(jnp.fft.fft2(wave) * kernel_conj)
        transmit = jnp.cos(phases[layer]) + 1j * jnp.sin(phases[layer])
        weighted = transmit[None] * (fields[layer, :, 0] + 1j * fields[layer, :, 1])
        slope_list.insert(0, lax.optimization_barrier(jnp.mean(jnp.imag(jnp.conj(weighted) * spread), axis=0)))
        wave = jnp.conj(transmit)[None] * spread
    slopes = jnp.stack(slope_list).astype(jnp.float32)
    adjoint_wave = jnp.stack([jnp.real(wave), jnp.imag(wave)], axis=1).astype(jnp.float32)
    return (slopes, adjoint_wave)
```

```python
import math

import jax
import jax.numpy as jnp
import numpy as np
from jax import lax
from jax.experimental import pallas as pl
from jax.experimental.pallas import tpu as pltpu
from jax.sharding import PartitionSpec as P

N = 1024
GRID = 15
DZ = 64
SHIFT = 10
LANES = 128
TILE = 8
VMEM_LIMIT = 58 * 1024 * 1024
ROWS = 16
PEERS = 64
GROUPS = 8
LEDS = 2
SLICES = 2
MESH = pl.DeviceIdType.MESH
F32 = jnp.float32
BF16 = jnp.bfloat16


def dft_block(length):
    index = np.arange(length)
    angle = 2.0 * np.pi * (np.outer(index, index) % length) / length
    return np.cos(angle), np.sin(angle)


def complex_left(length):
    cos, sin = dft_block(length)
    return np.block([[cos, sin], [-sin, cos]])


def tables():
    wide = complex_left(LANES).astype(np.float32)
    long = complex_left(PEERS).astype(np.float32)
    cos, sin = dft_block(ROWS)
    eye = np.eye(LANES // ROWS)
    cos, sin = np.kron(eye, cos), np.kron(eye, sin)
    short = np.block([[cos, -sin], [sin, cos]]).astype(np.float32)
    angle = 2.0 * np.pi * np.outer(np.arange(TILE), np.arange(LANES)) / N
    turn_rows = np.concatenate([np.cos(angle), np.sin(angle)]).astype(np.float32)
    angle = 2.0 * np.pi * np.outer(np.arange(PEERS), np.arange(LANES) % ROWS) / N
    turn_cols = np.stack([np.cos(angle), np.sin(angle)]).astype(np.float32)
    return wide, long, short, turn_rows, turn_cols


def fit_turns():
    nodes = 0.5 * np.cos(np.pi * (np.arange(400) + 0.5) / 800)
    square = nodes * nodes
    basis = np.vander(square, 8, increasing=True)
    sin_fit = np.linalg.lstsq(basis, np.sin(2 * np.pi * nodes) / nodes, rcond=None)[0]
    cos_fit = np.linalg.lstsq(basis, np.cos(2 * np.pi * nodes), rcond=None)[0]
    return [float(v) for v in sin_fit], [float(v) for v in cos_fit]


SIN_FIT, COS_FIT = fit_turns()


def cos_sin_turns(turns):
    frac = turns - jnp.floor(turns + 0.5)
    square = frac * frac
    sine = jnp.full_like(square, SIN_FIT[-1])
    cosine = jnp.full_like(square, COS_FIT[-1])
    for s, c in zip(SIN_FIT[-2::-1], COS_FIT[-2::-1]):
        sine = sine * square + s
        cosine = cosine * square + c
    return cosine, sine * frac


def split(value):
    high = value.astype(BF16)
    return high, (value - high.astype(F32)).astype(BF16)


def dot3(left, right, dims):
    def dot(a, b):
        return lax.dot_general(a, b, (dims, ((), ())), preferred_element_type=F32)

    return dot(left[0], right[0]) + (dot(left[0], right[1]) + dot(left[1], right[0]))


def radix8(real, imag):
    half = math.sqrt(0.5)

    def pair(a, b):
        return (a[0] + b[0], a[1] + b[1]), (a[0] - b[0], a[1] - b[1])

    def minus_i(a):
        return a[1], -a[0]

    def four(z):
        s0, d0 = pair(z[0], z[2])
        s1, d1 = pair(z[1], z[3])
        y0, y2 = pair(s0, s1)
        y1, y3 = pair(d0, minus_i(d1))
        return [y0, y1, y2, y3]

    z = list(zip(real, imag))
    even = four([z[0], z[2], z[4], z[6]])
    odd = four([z[1], z[3], z[5], z[7]])
    odd[1] = ((odd[1][0] + odd[1][1]) * half, (odd[1][1] - odd[1][0]) * half)
    odd[2] = minus_i(odd[2])
    odd[3] = ((odd[3][1] - odd[3][0]) * half, (odd[3][0] + odd[3][1]) * -half)
    out = [None] * 8
    for k in range(4):
        out[k], out[k + 4] = pair(even[k], odd[k])
    return [o[0] for o in out], [o[1] for o in out]


def twist(real, imag, cos, sin):
    return real * cos + imag * sin, imag * cos - real * sin


def row_forward(real, imag, turn_cos, turn_sin, wide):
    real, imag = radix8(real, imag)
    rows = []
    for k in range(8):
        re, im = (real[k], imag[k]) if k == 0 else twist(real[k], imag[k], turn_cos[k], turn_sin[k])
        rows.append(jnp.concatenate([re, im], axis=1))
    return dot3(wide, split(jnp.concatenate(rows, axis=0)), ((1,), (1,)))


def row_inverse(swapped, turn_cos, turn_sin, wide):
    spread = dot3(wide, split(swapped), ((1,), (0,)))
    first = spread[:LANES].T
    second = spread[LANES:].T
    real, imag = [], []
    for k in range(8):
        re, im = first[ROWS * k : ROWS * (k + 1)], second[ROWS * k : ROWS * (k + 1)]
        if k > 0:
            re, im = twist(re, im, turn_cos[k], turn_sin[k])
        real.append(re)
        imag.append(im)
    return radix8(real, imag)


def column_forward(blocks, turn_cos, turn_sin, long, short):
    stacked = jnp.concatenate([jnp.concatenate(blocks[c], axis=1) for c in range(2)], axis=0)
    mixed = dot3(long, split(stacked), ((1,), (0,)))
    rows = []
    for k in range(2):
        re = mixed[:PEERS, LANES * k : LANES * (k + 1)]
        im = mixed[PEERS:, LANES * k : LANES * (k + 1)]
        rows.append(jnp.concatenate(twist(re, im, turn_cos, turn_sin), axis=1))
    return dot3(split(jnp.concatenate(rows, axis=0)), short, ((1,), (0,)))


def column_inverse(real, imag, turn_cos, turn_sin, long, short):
    mixed = dot3(split(jnp.concatenate([real, imag], axis=1)), short, ((1,), (0,)))
    first, second = [], []
    for k in range(2):
        block = mixed[PEERS * k : PEERS * (k + 1)]
        re, im = twist(block[:, :LANES], block[:, LANES:], turn_cos, turn_sin)
        first.append(re)
        second.append(im)
    stacked = jnp.concatenate(
        [jnp.concatenate(first, axis=1), jnp.concatenate(second, axis=1)], axis=0
    )
    return dot3(long, split(stacked), ((1,), (0,)))


def filter_block(owner, k2lo, led):
    lane = lax.broadcasted_iota(jnp.int32, (PEERS, LANES), 1)
    v1 = lax.broadcasted_iota(jnp.int32, (PEERS, LANES), 0)
    u = (lane >> 4) + 8 * (PEERS * k2lo + owner)
    v = v1 + PEERS * (lane & (ROWS - 1))
    kx = (led // GRID - GRID // 2) * SHIFT
    ky = (led % GRID - GRID // 2) * SHIFT
    fx = (((u + N // 2) & (N - 1)) - N // 2 + kx).astype(F32) * (1.0 / N)
    fy = (((v + N // 2) & (N - 1)) - N // 2 + ky).astype(F32) * (1.0 / N)
    turns = DZ * (jnp.sqrt(1.0 - fx * fx - fy * fy) - 1.0)
    cosine, sine = cos_sin_turns(turns)
    return cosine * (1.0 / (N * N)), sine * (1.0 / (N * N))


def kernel(
    led_ref, fields_hbm, phases_hbm, residual_hbm, wide_hbm, long_hbm, short_hbm, trow_hbm, tcol_hbm,
    slopes_hbm, wave_hbm,
    fields, phases, wave, wide_f32, long_f32, short_f32, trow, tcol, wide_ref, long_ref, short_ref,
    filt, trans, out_box, in_box, slope_out, slope_in, slopes,
    load_sem, send_sem, recv_sem, lsend_sem, lrecv_sem, store_sem,
):
    me = lax.axis_index("row")
    group = lax.axis_index("led")
    my_y, my_w = me // 8, me % 8
    led_peers = [lax.rem(group + d, GROUPS) for d in (4, 3, 5, 2, 6, 7, 1)]

    loads = [
        pltpu.make_async_copy(src, dst, load_sem.at[n])
        for n, (src, dst) in enumerate(
            [
                (residual_hbm, wave),
                (trow_hbm, trow),
                (wide_hbm, wide_f32),
                (tcol_hbm, tcol),
                (long_hbm, long_f32),
                (short_hbm, short_f32),
                (phases_hbm, phases),
                (fields_hbm, fields),
            ]
        )
    ]
    for load in loads:
        load.start()

    barrier = pltpu.get_barrier_semaphore()

    @pl.loop(1, PEERS)
    def _(step):
        peer = lax.rem(me + step, PEERS)
        pl.semaphore_signal(barrier, inc=1, device_id=(group, peer), device_id_type=MESH)

    for peer in led_peers:
        pl.semaphore_signal(barrier, inc=1, device_id=(peer, me), device_id_type=MESH)

    for load in loads[:3]:
        load.wait()
    turn_cos = [trow[k : k + 1, :] for k in range(8)]
    turn_sin = [trow[8 + k : 9 + k, :] for k in range(8)]
    wide_ref[0], wide_ref[1] = split(wide_f32[...])

    def halves(table):
        return table[0], table[1]

    bases = [lax.rem(my_y + dy, 8) * 8 for dy in range(8)]

    def send_tile(slot, peer):
        pltpu.make_async_remote_copy(
            src_ref=out_box.at[slot, peer],
            dst_ref=in_box.at[slot, me],
            send_sem=send_sem.at[slot],
            recv_sem=recv_sem.at[slot],
            device_id=(group, peer),
            device_id_type=MESH,
        ).start()

    def send(slot):
        @pl.loop(1, 8)
        def _(dw):
            column = lax.rem(my_w + dw, 8)
            for dy in (4, 3, 5, 2, 6, 1, 7, 0):
                send_tile(slot, bases[dy] + column)

        for dy in (4, 3, 5, 2, 6, 1, 7):
            send_tile(slot, bases[dy] + my_w)
        pltpu.make_async_copy(out_box.at[slot, me], in_box.at[slot, me], recv_sem.at[slot]).start()

    def put(values, slot):
        flat = out_box.at[slot].reshape(PEERS * 4, LANES)
        for j in range(4):
            flat[pl.ds(j, PEERS, stride=4), :] = values[j]

    def arrived(slot):
        whole = in_box.at[slot]
        pltpu.make_async_copy(whole, whole, recv_sem.at[slot]).wait()
        flat = whole.reshape(PEERS * 4, LANES)
        return [flat[pl.ds(j, PEERS, stride=4), :] for j in range(4)]

    def columns_of(ref, c):
        return [ref[c, :, LANES * a : LANES * (a + 1)] for a in range(8)]

    def to_columns(led, slot):
        seed = wave.at[led]
        spectrum = row_forward(
            columns_of(seed, 0), columns_of(seed, 1), turn_cos, turn_sin, halves(wide_ref)
        )
        put([spectrum[PEERS * j : PEERS * (j + 1)] for j in range(4)], slot)

    def slot_of(turn, way, led):
        return (2 * turn + way) * LEDS + led

    def column_pass(turn, led):
        tiles = arrived(slot_of(turn, 0, led))
        spectrum = column_forward([tiles[:2], tiles[2:]], tcol[0], tcol[1], halves(long_ref), halves(short_ref))
        real, imag = twist(spectrum[:, :LANES], spectrum[:, LANES:], filt[led, 0], filt[led, 1])
        back = column_inverse(imag, real, tcol[0], tcol[1], halves(long_ref), halves(short_ref))
        values = [
            back[PEERS * (1 - c) : PEERS * (2 - c), LANES * k : LANES * (k + 1)]
            for c in range(2)
            for k in range(2)
        ]
        put(values, slot_of(turn, 1, led))
        send(slot_of(turn, 1, led))

    def send_slopes(turn):
        for peer in led_peers:
            pltpu.make_async_remote_copy(
                src_ref=slope_out.at[turn, peer],
                dst_ref=slope_in.at[turn, group],
                send_sem=lsend_sem.at[turn],
                recv_sem=lrecv_sem.at[turn],
                device_id=(peer, me),
                device_id_type=MESH,
            ).start()
        pltpu.make_async_copy(
            slope_out.at[turn, group], slope_in.at[turn, group], lrecv_sem.at[turn]
        ).start()

    def from_columns(turn, led):
        layer = SLICES - 1 - turn
        tiles = arrived(slot_of(turn, 1, led))
        swapped = jnp.concatenate([tiles[2], tiles[3], tiles[0], tiles[1]], axis=0)
        imag, real = row_inverse(swapped, turn_cos, turn_sin, halves(wide_ref))
        for a in range(8):
            cols = slice(LANES * a, LANES * (a + 1))
            re, im = twist(real[a], imag[a], trans[layer, 0, :, cols], trans[layer, 1, :, cols])
            wave[led, 0, :, cols] = re
            wave[led, 1, :, cols] = im

    def slope_terms(turn, led):
        layer = SLICES - 1 - turn
        for a in range(8):
            cols = slice(LANES * a, LANES * (a + 1))
            slope_out[turn, a] += (
                fields[layer, led, 0, :, cols] * wave[led, 1, :, cols]
                - fields[layer, led, 1, :, cols] * wave[led, 0, :, cols]
            )

    slope_out[...] = jnp.zeros_like(slope_out)

    @pl.loop(0, SLICES + 1)
    def _(phase):
        @pl.loop(0, LEDS)
        def _(led):
            @pl.when(phase > 0)
            def _():
                from_columns(phase - 1, led)

            @pl.when(phase < SLICES)
            def _():
                to_columns(led, slot_of(phase, 0, led))

                @pl.when(phase + led == 0)
                def _():
                    pl.semaphore_wait(barrier, PEERS - 1 + GROUPS - 1)

                send(slot_of(phase, 0, led))

            @pl.when(phase > 0)
            def _():
                slope_terms(phase - 1, led)

                @pl.when(led == LEDS - 1)
                def _():
                    send_slopes(phase - 1)

            @pl.when(phase == SLICES)
            def _():
                pltpu.make_async_copy(wave.at[led], wave_hbm.at[led], store_sem.at[led]).start()

        @pl.when(phase == 0)
        def _():
            for led in range(LEDS):
                for k in range(2):
                    cosine, sine = filter_block(me, k, led_ref[led])
                    filt[led, 0, PEERS * k : PEERS * (k + 1), :] = cosine
                    filt[led, 1, PEERS * k : PEERS * (k + 1), :] = sine
            for load in loads[3:]:
                load.wait()
            long_ref[0], long_ref[1] = split(long_f32[...])
            short_ref[0], short_ref[1] = split(short_f32[...])
            for layer in range(SLICES):
                cosine, sine = cos_sin_turns(phases[layer] * (0.5 / math.pi))
                trans[layer, 0] = cosine
                trans[layer, 1] = sine

        @pl.when(phase < SLICES)
        def _():
            @pl.loop(0, LEDS)
            def _(led):
                column_pass(phase, led)

    for turn in range(SLICES):
        pltpu.make_async_copy(slope_in.at[turn], slope_in.at[turn], lrecv_sem.at[turn]).wait()
        slopes[SLICES - 1 - turn] = jnp.sum(slope_in[turn], axis=0) * (1.0 / (LEDS * GROUPS))
    store_slopes = pltpu.make_async_copy(slopes, slopes_hbm, store_sem.at[LEDS])
    store_slopes.start()
    for slot in range(2 * SLICES * LEDS):
        sent = out_box.at[slot, pl.ds(0, PEERS - 1)]
        pltpu.make_async_copy(sent, sent, send_sem.at[slot]).wait()
    for turn in range(SLICES):
        sent = slope_out.at[turn, pl.ds(0, GROUPS - 1)]
        pltpu.make_async_copy(sent, sent, lsend_sem.at[turn]).wait()
    for led in range(LEDS):
        pltpu.make_async_copy(wave.at[led], wave_hbm.at[led], store_sem.at[led]).wait()
    store_slopes.wait()


def local(fields, phases, residual, led_index):
    consts = [jnp.asarray(t) for t in tables()]
    scratch = [
        pltpu.VMEM(fields.shape, F32),
        pltpu.VMEM(phases.shape, F32),
        pltpu.VMEM(residual.shape, F32),
    ]
    slots = 2 * SLICES * LEDS
    scratch += [pltpu.VMEM(t.shape, t.dtype) for t in consts]
    scratch += [pltpu.VMEM((2,) + t.shape, BF16) for t in consts[:3]]
    scratch += [
        pltpu.VMEM((LEDS, 2, LANES, LANES), F32),
        pltpu.VMEM((SLICES, 2, ROWS, N), F32),
    ]
    scratch += [pltpu.VMEM((slots, PEERS, 4, LANES), F32)] * 2
    scratch += [
        pltpu.VMEM((SLICES, GROUPS, ROWS, LANES), F32),
        pltpu.VMEM((SLICES, GROUPS, ROWS, LANES), F32),
        pltpu.VMEM((SLICES, ROWS, LANES), F32),
        pltpu.SemaphoreType.DMA((8,)),
        pltpu.SemaphoreType.DMA((slots,)),
        pltpu.SemaphoreType.DMA((slots,)),
        pltpu.SemaphoreType.DMA((SLICES,)),
        pltpu.SemaphoreType.DMA((SLICES,)),
        pltpu.SemaphoreType.DMA((LEDS + 1,)),
    ]
    anywhere = pl.BlockSpec(memory_space=pl.ANY)
    return pl.pallas_call(
        kernel,
        out_shape=(
            jax.ShapeDtypeStruct((SLICES, ROWS, LANES), F32),
            jax.ShapeDtypeStruct(residual.shape, F32),
        ),
        in_specs=[pl.BlockSpec(memory_space=pltpu.SMEM)] + [anywhere] * 8,
        out_specs=(anywhere, anywhere),
        scratch_shapes=scratch,
        compiler_params=pltpu.CompilerParams(
            collective_id=0, has_side_effects=True, vmem_limit_bytes=VMEM_LIMIT
        ),
        name="adjoint",
    )(led_index, fields, phases, residual, *consts)


def solution(mesh):
    in_specs = (
        P(None, "led", None, "row", None),
        P(None, "row", None),
        P("led", None, "row", None),
        P("led"),
    )
    out_specs = (P(None, "row", "led"), P("led", None, "row", None))
    return jax.shard_map(local, mesh=mesh, in_specs=in_specs, out_specs=out_specs, check_vma=False)
```

```python
import math

import jax
import jax.numpy as jnp
import numpy as np
from jax import lax
from jax.experimental import pallas as pl
from jax.experimental.pallas import tpu as pltpu
from jax.sharding import PartitionSpec as P

N = 1024
GRID = 15
DZ = 64
SHIFT = 10
LANES = 128
TILE = 8
VMEM_LIMIT = 40 * 1024 * 1024
ROWS = 16
PEERS = 64
GROUPS = 8
LEDS = 2
SLICES = 2
MESH = pl.DeviceIdType.MESH
F32 = jnp.float32
BF16 = jnp.bfloat16


def dft_block(length):
    index = np.arange(length)
    angle = 2.0 * np.pi * (np.outer(index, index) % length) / length
    return np.cos(angle), np.sin(angle)


def complex_left(length):
    cos, sin = dft_block(length)
    return np.block([[cos, sin], [-sin, cos]])


def tables():
    wide = complex_left(LANES).astype(np.float32)
    long = complex_left(PEERS).astype(np.float32)
    cos, sin = dft_block(ROWS)
    eye = np.eye(LANES // ROWS)
    cos, sin = np.kron(eye, cos), np.kron(eye, sin)
    short = np.block([[cos, -sin], [sin, cos]]).astype(np.float32)
    angle = 2.0 * np.pi * np.outer(np.arange(TILE), np.arange(LANES)) / N
    turn_rows = np.concatenate([np.cos(angle), np.sin(angle)]).astype(np.float32)
    angle = 2.0 * np.pi * np.outer(np.arange(PEERS), np.arange(LANES) % ROWS) / N
    turn_cols = np.stack([np.cos(angle), np.sin(angle)]).astype(np.float32)
    return wide, long, short, turn_rows, turn_cols


def fit_turns():
    nodes = 0.5 * np.cos(np.pi * (np.arange(400) + 0.5) / 800)
    square = nodes * nodes
    basis = np.vander(square, 8, increasing=True)
    sin_fit = np.linalg.lstsq(basis, np.sin(2 * np.pi * nodes) / nodes, rcond=None)[0]
    cos_fit = np.linalg.lstsq(basis, np.cos(2 * np.pi * nodes), rcond=None)[0]
    return [float(v) for v in sin_fit], [float(v) for v in cos_fit]


SIN_FIT, COS_FIT = fit_turns()


def cos_sin_turns(turns):
    frac = turns - jnp.floor(turns + 0.5)
    square = frac * frac
    sine = jnp.full_like(square, SIN_FIT[-1])
    cosine = jnp.full_like(square, COS_FIT[-1])
    for s, c in zip(SIN_FIT[-2::-1], COS_FIT[-2::-1]):
        sine = sine * square + s
        cosine = cosine * square + c
    return cosine, sine * frac


def split(value):
    high = value.astype(BF16)
    return high, (value - high.astype(F32)).astype(BF16)


def dot3(left, right, dims):
    def dot(a, b):
        return lax.dot_general(a, b, (dims, ((), ())), preferred_element_type=F32)

    return dot(left[0], right[0]) + (dot(left[0], right[1]) + dot(left[1], right[0]))


def radix8(real, imag):
    half = math.sqrt(0.5)

    def pair(a, b):
        return (a[0] + b[0], a[1] + b[1]), (a[0] - b[0], a[1] - b[1])

    def minus_i(a):
        return a[1], -a[0]

    def four(z):
        s0, d0 = pair(z[0], z[2])
        s1, d1 = pair(z[1], z[3])
        y0, y2 = pair(s0, s1)
        y1, y3 = pair(d0, minus_i(d1))
        return [y0, y1, y2, y3]

    z = list(zip(real, imag))
    even = four([z[0], z[2], z[4], z[6]])
    odd = four([z[1], z[3], z[5], z[7]])
    odd[1] = ((odd[1][0] + odd[1][1]) * half, (odd[1][1] - odd[1][0]) * half)
    odd[2] = minus_i(odd[2])
    odd[3] = ((odd[3][1] - odd[3][0]) * half, (odd[3][0] + odd[3][1]) * -half)
    out = [None] * 8
    for k in range(4):
        out[k], out[k + 4] = pair(even[k], odd[k])
    return [o[0] for o in out], [o[1] for o in out]


def twist(real, imag, cos, sin):
    return real * cos + imag * sin, imag * cos - real * sin


def row_forward(real, imag, turn_cos, turn_sin, wide):
    real, imag = radix8(real, imag)
    rows = []
    for k in range(8):
        re, im = (real[k], imag[k]) if k == 0 else twist(real[k], imag[k], turn_cos[k], turn_sin[k])
        rows.append(jnp.concatenate([re, im], axis=1))
    return dot3(wide, split(jnp.concatenate(rows, axis=0)), ((1,), (1,)))


def row_inverse(swapped, turn_cos, turn_sin, wide):
    spread = dot3(wide, split(swapped), ((1,), (0,)))
    first = spread[:LANES].T
    second = spread[LANES:].T
    real, imag = [], []
    for k in range(8):
        re, im = first[ROWS * k : ROWS * (k + 1)], second[ROWS * k : ROWS * (k + 1)]
        if k > 0:
            re, im = twist(re, im, turn_cos[k], turn_sin[k])
        real.append(re)
        imag.append(im)
    return radix8(real, imag)


def column_forward(blocks, turn_cos, turn_sin, long, short):
    stacked = jnp.concatenate([jnp.concatenate(blocks[c], axis=1) for c in range(2)], axis=0)
    mixed = dot3(long, split(stacked), ((1,), (0,)))
    rows = []
    for k in range(2):
        re = mixed[:PEERS, LANES * k : LANES * (k + 1)]
        im = mixed[PEERS:, LANES * k : LANES * (k + 1)]
        rows.append(jnp.concatenate(twist(re, im, turn_cos, turn_sin), axis=1))
    return dot3(split(jnp.concatenate(rows, axis=0)), short, ((1,), (0,)))


def column_inverse(real, imag, turn_cos, turn_sin, long, short):
    mixed = dot3(split(jnp.concatenate([real, imag], axis=1)), short, ((1,), (0,)))
    first, second = [], []
    for k in range(2):
        block = mixed[PEERS * k : PEERS * (k + 1)]
        re, im = twist(block[:, :LANES], block[:, LANES:], turn_cos, turn_sin)
        first.append(re)
        second.append(im)
    stacked = jnp.concatenate(
        [jnp.concatenate(first, axis=1), jnp.concatenate(second, axis=1)], axis=0
    )
    return dot3(long, split(stacked), ((1,), (0,)))


def filter_block(owner, k2lo, led):
    lane = lax.broadcasted_iota(jnp.int32, (PEERS, LANES), 1)
    v1 = lax.broadcasted_iota(jnp.int32, (PEERS, LANES), 0)
    u = (lane >> 4) + 8 * (PEERS * k2lo + owner)
    v = v1 + PEERS * (lane & (ROWS - 1))
    kx = (led // GRID - GRID // 2) * SHIFT
    ky = (led % GRID - GRID // 2) * SHIFT
    fx = (((u + N // 2) & (N - 1)) - N // 2 + kx).astype(F32) * (1.0 / N)
    fy = (((v + N // 2) & (N - 1)) - N // 2 + ky).astype(F32) * (1.0 / N)
    turns = DZ * (jnp.sqrt(1.0 - fx * fx - fy * fy) - 1.0)
    cosine, sine = cos_sin_turns(turns)
    return cosine * (1.0 / (N * N)), sine * (1.0 / (N * N))


def kernel(
    led_hbm, fields_hbm, phases_hbm, residual_hbm, wide_hbm, long_hbm, short_hbm, trow_hbm, tcol_hbm,
    slopes, wave,
    led_ref, fields, phases, wide_f32, long_f32, short_f32, trow, tcol, wide_ref, long_ref, short_ref,
    filt, trans, out_box, in_box, slope_out, slope_in,
    load_sem, send_sem, recv_sem, lsend_sem, lrecv_sem,
):
    me = lax.axis_index("row")
    group = lax.axis_index("led")
    my_y, my_w = me // 8, me % 8
    led_peers = [lax.rem(group + d, GROUPS) for d in (4, 3, 5, 2, 6, 7, 1)]

    loads = [
        pltpu.make_async_copy(src, dst, load_sem.at[n])
        for n, (src, dst) in enumerate(
            [
                (residual_hbm, wave),
                (trow_hbm, trow),
                (wide_hbm, wide_f32),
                (tcol_hbm, tcol),
                (long_hbm, long_f32),
                (short_hbm, short_f32),
                (phases_hbm, phases),
                (fields_hbm, fields),
                (led_hbm, led_ref),
            ]
        )
    ]
    for load in loads:
        load.start()

    barrier = pltpu.get_barrier_semaphore()

    @pl.loop(1, PEERS)
    def _(step):
        peer = lax.rem(me + step, PEERS)
        pl.semaphore_signal(barrier, inc=1, device_id=(group, peer), device_id_type=MESH)

    for peer in led_peers:
        pl.semaphore_signal(barrier, inc=1, device_id=(peer, me), device_id_type=MESH)

    for load in loads[:3]:
        load.wait()
    turn_cos = [trow[k : k + 1, :] for k in range(8)]
    turn_sin = [trow[8 + k : 9 + k, :] for k in range(8)]
    wide_ref[0], wide_ref[1] = split(wide_f32[...])

    def halves(table):
        return table[0], table[1]

    bases = [lax.rem(my_y + dy, 8) * 8 for dy in range(8)]

    def send_tile(slot, peer):
        pltpu.make_async_remote_copy(
            src_ref=out_box.at[slot, peer],
            dst_ref=in_box.at[slot, me],
            send_sem=send_sem.at[slot],
            recv_sem=recv_sem.at[slot],
            device_id=(group, peer),
            device_id_type=MESH,
        ).start()

    columns = [lax.rem(my_w + dw, 8) for dw in range(8)]

    def send(slot):
        for dw in (5, 4, 3, 1, 7, 2, 6, 0):
            for dy in (4, 3, 5, 2, 6, 1, 7, 0):
                if dw + dy > 0:
                    send_tile(slot, bases[dy] + columns[dw])
        pltpu.make_async_copy(out_box.at[slot, me], in_box.at[slot, me], recv_sem.at[slot]).start()

    def put(values, slot):
        flat = out_box.at[slot].reshape(PEERS * 4, LANES)
        for j in range(4):
            flat[pl.ds(j, PEERS, stride=4), :] = values[j]

    def arrived(slot):
        whole = in_box.at[slot]
        pltpu.make_async_copy(whole, whole, recv_sem.at[slot]).wait()
        flat = whole.reshape(PEERS * 4, LANES)
        return [flat[pl.ds(j, PEERS, stride=4), :] for j in range(4)]

    def columns_of(ref, c):
        return [ref[c, :, LANES * a : LANES * (a + 1)] for a in range(8)]

    def to_columns(led, slot):
        seed = wave.at[led]
        spectrum = row_forward(
            columns_of(seed, 0), columns_of(seed, 1), turn_cos, turn_sin, halves(wide_ref)
        )
        put([spectrum[PEERS * j : PEERS * (j + 1)] for j in range(4)], slot)

    def slot_of(turn, way, led):
        return (2 * turn + way) * LEDS + led

    def column_pass(turn, led):
        tiles = arrived(slot_of(turn, 0, led))
        spectrum = column_forward([tiles[:2], tiles[2:]], tcol[0], tcol[1], halves(long_ref), halves(short_ref))
        real, imag = twist(spectrum[:, :LANES], spectrum[:, LANES:], filt[led, 0], filt[led, 1])
        back = column_inverse(imag, real, tcol[0], tcol[1], halves(long_ref), halves(short_ref))
        values = [
            back[PEERS * (1 - c) : PEERS * (2 - c), LANES * k : LANES * (k + 1)]
            for c in range(2)
            for k in range(2)
        ]
        put(values, slot_of(turn, 1, led))
        send(slot_of(turn, 1, led))

    def send_slopes(turn):
        for peer in led_peers:
            pltpu.make_async_remote_copy(
                src_ref=slope_out.at[turn, peer],
                dst_ref=slope_in.at[turn, group],
                send_sem=lsend_sem.at[turn],
                recv_sem=lrecv_sem.at[turn],
                device_id=(peer, me),
                device_id_type=MESH,
            ).start()
        pltpu.make_async_copy(
            slope_out.at[turn, group], slope_in.at[turn, group], lrecv_sem.at[turn]
        ).start()

    def from_columns(turn, led):
        layer = SLICES - 1 - turn
        tiles = arrived(slot_of(turn, 1, led))
        swapped = jnp.concatenate([tiles[2], tiles[3], tiles[0], tiles[1]], axis=0)
        imag, real = row_inverse(swapped, turn_cos, turn_sin, halves(wide_ref))
        for a in range(8):
            cols = slice(LANES * a, LANES * (a + 1))
            re, im = twist(real[a], imag[a], trans[layer, 0, :, cols], trans[layer, 1, :, cols])
            wave[led, 0, :, cols] = re
            wave[led, 1, :, cols] = im

    def slope_terms(turn, led):
        layer = SLICES - 1 - turn
        for a in range(8):
            cols = slice(LANES * a, LANES * (a + 1))
            slope_out[turn, a] += (
                fields[layer, led, 0, :, cols] * wave[led, 1, :, cols]
                - fields[layer, led, 1, :, cols] * wave[led, 0, :, cols]
            )

    slope_out[...] = jnp.zeros_like(slope_out)

    @pl.loop(0, SLICES + 1)
    def _(phase):
        @pl.loop(0, LEDS)
        def _(led):
            @pl.when(phase > 0)
            def _():
                from_columns(phase - 1, led)

            @pl.when(phase < SLICES)
            def _():
                to_columns(led, slot_of(phase, 0, led))

                @pl.when(phase + led == 0)
                def _():
                    pl.semaphore_wait(barrier, PEERS - 1 + GROUPS - 1)

                send(slot_of(phase, 0, led))

            @pl.when(phase > 0)
            def _():
                slope_terms(phase - 1, led)

                @pl.when(led == LEDS - 1)
                def _():
                    send_slopes(phase - 1)

        @pl.when(phase == 0)
        def _():
            for load in loads[3:]:
                load.wait()
            for led in range(LEDS):
                for k in range(2):
                    cosine, sine = filter_block(me, k, led_ref[led])
                    filt[led, 0, PEERS * k : PEERS * (k + 1), :] = cosine
                    filt[led, 1, PEERS * k : PEERS * (k + 1), :] = sine
            long_ref[0], long_ref[1] = split(long_f32[...])
            short_ref[0], short_ref[1] = split(short_f32[...])
            for layer in range(SLICES):
                cosine, sine = cos_sin_turns(phases[layer] * (0.5 / math.pi))
                trans[layer, 0] = cosine
                trans[layer, 1] = sine

        @pl.when(phase < SLICES)
        def _():
            @pl.loop(0, LEDS)
            def _(led):
                column_pass(phase, led)

    for turn in range(SLICES):
        pltpu.make_async_copy(slope_in.at[turn], slope_in.at[turn], lrecv_sem.at[turn]).wait()
        slopes[SLICES - 1 - turn] = jnp.sum(slope_in[turn], axis=0) * (1.0 / (LEDS * GROUPS))
    for slot in range(2 * SLICES * LEDS):
        sent = out_box.at[slot, pl.ds(0, PEERS - 1)]
        pltpu.make_async_copy(sent, sent, send_sem.at[slot]).wait()
    for turn in range(SLICES):
        sent = slope_out.at[turn, pl.ds(0, GROUPS - 1)]
        pltpu.make_async_copy(sent, sent, lsend_sem.at[turn]).wait()


def local(fields, phases, residual, led_index):
    consts = [jnp.asarray(t) for t in tables()]
    scratch = [
        pltpu.SMEM(led_index.shape, jnp.int32),
        pltpu.VMEM(fields.shape, F32),
        pltpu.VMEM(phases.shape, F32),
    ]
    slots = 2 * SLICES * LEDS
    scratch += [pltpu.VMEM(t.shape, t.dtype) for t in consts]
    scratch += [pltpu.VMEM((2,) + t.shape, BF16) for t in consts[:3]]
    scratch += [
        pltpu.VMEM((LEDS, 2, LANES, LANES), F32),
        pltpu.VMEM((SLICES, 2, ROWS, N), F32),
    ]
    scratch += [pltpu.VMEM((slots, PEERS, 4, LANES), F32)] * 2
    scratch += [
        pltpu.VMEM((SLICES, GROUPS, ROWS, LANES), F32),
        pltpu.VMEM((SLICES, GROUPS, ROWS, LANES), F32),
        pltpu.SemaphoreType.DMA((9,)),
        pltpu.SemaphoreType.DMA((slots,)),
        pltpu.SemaphoreType.DMA((slots,)),
        pltpu.SemaphoreType.DMA((SLICES,)),
        pltpu.SemaphoreType.DMA((SLICES,)),
    ]
    held = [
        pltpu.with_memory_space_constraint(x, pltpu.HBM) for x in [led_index, fields, phases, residual] + consts
    ]
    anywhere = pl.BlockSpec(memory_space=pl.ANY)
    return pl.pallas_call(
        kernel,
        out_shape=(
            pltpu.VMEM((SLICES, ROWS, LANES), F32),
            pltpu.VMEM(residual.shape, F32),
        ),
        in_specs=[anywhere] * 9,
        out_specs=(pl.BlockSpec(memory_space=pltpu.VMEM),) * 2,
        scratch_shapes=scratch,
        compiler_params=pltpu.CompilerParams(
            collective_id=0, has_side_effects=True, vmem_limit_bytes=VMEM_LIMIT
        ),
        name="adjoint",
    )(*held)


def solution(mesh):
    in_specs = (
        P(None, "led", None, "row", None),
        P(None, "row", None),
        P("led", None, "row", None),
        P("led"),
    )
    out_specs = (P(None, "row", "led"), P("led", None, "row", None))
    return jax.shard_map(local, mesh=mesh, in_specs=in_specs, out_specs=out_specs, check_vma=False)
```

```python
import math

import jax
import jax.numpy as jnp
import numpy as np
from jax import lax
from jax.experimental import pallas as pl
from jax.experimental.pallas import tpu as pltpu
from jax.sharding import PartitionSpec as P

N = 1024
GRID = 15
DZ = 64
SHIFT = 10
LANES = 128
TILE = 8
VMEM_LIMIT = 40 * 1024 * 1024
ROWS = 16
PEERS = 64
OWNERS = 32
GROUPS = 8
LEDS = 2
SLICES = 2
MESH = pl.DeviceIdType.MESH
F32 = jnp.float32
BF16 = jnp.bfloat16


def dft_block(length):
    index = np.arange(length)
    angle = 2.0 * np.pi * (np.outer(index, index) % length) / length
    return np.cos(angle), np.sin(angle)


def complex_left(length):
    cos, sin = dft_block(length)
    return np.block([[cos, sin], [-sin, cos]])


def tables():
    wide = complex_left(LANES).astype(np.float32)
    long = complex_left(PEERS).astype(np.float32)
    cos, sin = dft_block(ROWS)
    eye = np.eye(LANES // ROWS)
    cos, sin = np.kron(eye, cos), np.kron(eye, sin)
    short = np.block([[cos, -sin], [sin, cos]]).astype(np.float32)
    angle = 2.0 * np.pi * np.outer(np.arange(TILE), np.arange(LANES)) / N
    turn_rows = np.concatenate([np.cos(angle), np.sin(angle)]).astype(np.float32)
    angle = 2.0 * np.pi * np.outer(np.arange(PEERS), np.arange(LANES) % ROWS) / N
    turn_cols = np.stack([np.cos(angle), np.sin(angle)]).astype(np.float32)
    return wide, long, short, turn_rows, turn_cols


def fit_turns():
    nodes = 0.5 * np.cos(np.pi * (np.arange(400) + 0.5) / 800)
    square = nodes * nodes
    basis = np.vander(square, 8, increasing=True)
    sin_fit = np.linalg.lstsq(basis, np.sin(2 * np.pi * nodes) / nodes, rcond=None)[0]
    cos_fit = np.linalg.lstsq(basis, np.cos(2 * np.pi * nodes), rcond=None)[0]
    return [float(v) for v in sin_fit], [float(v) for v in cos_fit]


SIN_FIT, COS_FIT = fit_turns()


def cos_sin_turns(turns):
    frac = turns - jnp.floor(turns + 0.5)
    square = frac * frac
    sine = jnp.full_like(square, SIN_FIT[-1])
    cosine = jnp.full_like(square, COS_FIT[-1])
    for s, c in zip(SIN_FIT[-2::-1], COS_FIT[-2::-1]):
        sine = sine * square + s
        cosine = cosine * square + c
    return cosine, sine * frac


def split(value):
    high = value.astype(BF16)
    return high, (value - high.astype(F32)).astype(BF16)


def dot3(left, right, dims):
    def dot(a, b):
        return lax.dot_general(a, b, (dims, ((), ())), preferred_element_type=F32)

    return dot(left[0], right[0]) + (dot(left[0], right[1]) + dot(left[1], right[0]))


def radix8(real, imag):
    half = math.sqrt(0.5)

    def pair(a, b):
        return (a[0] + b[0], a[1] + b[1]), (a[0] - b[0], a[1] - b[1])

    def minus_i(a):
        return a[1], -a[0]

    def four(z):
        s0, d0 = pair(z[0], z[2])
        s1, d1 = pair(z[1], z[3])
        y0, y2 = pair(s0, s1)
        y1, y3 = pair(d0, minus_i(d1))
        return [y0, y1, y2, y3]

    z = list(zip(real, imag))
    even = four([z[0], z[2], z[4], z[6]])
    odd = four([z[1], z[3], z[5], z[7]])
    odd[1] = ((odd[1][0] + odd[1][1]) * half, (odd[1][1] - odd[1][0]) * half)
    odd[2] = minus_i(odd[2])
    odd[3] = ((odd[3][1] - odd[3][0]) * half, (odd[3][0] + odd[3][1]) * -half)
    out = [None] * 8
    for k in range(4):
        out[k], out[k + 4] = pair(even[k], odd[k])
    return [o[0] for o in out], [o[1] for o in out]


def twist(real, imag, cos, sin):
    return real * cos + imag * sin, imag * cos - real * sin


def row_forward(real, imag, turn_cos, turn_sin, wide):
    real, imag = radix8(real, imag)
    rows = []
    for k in range(8):
        re, im = (real[k], imag[k]) if k == 0 else twist(real[k], imag[k], turn_cos[k], turn_sin[k])
        rows.append(jnp.concatenate([re, im], axis=1))
    return dot3(wide, split(jnp.concatenate(rows, axis=0)), ((1,), (1,)))


def row_inverse(swapped, turn_cos, turn_sin, wide):
    spread = dot3(wide, split(swapped), ((1,), (0,)))
    first = spread[:LANES].T
    second = spread[LANES:].T
    real, imag = [], []
    for k in range(8):
        re, im = first[ROWS * k : ROWS * (k + 1)], second[ROWS * k : ROWS * (k + 1)]
        if k > 0:
            re, im = twist(re, im, turn_cos[k], turn_sin[k])
        real.append(re)
        imag.append(im)
    return radix8(real, imag)


def column_forward(blocks, turn_cos, turn_sin, long, short):
    stacked = jnp.concatenate([jnp.concatenate(blocks[c], axis=1) for c in range(2)], axis=0)
    mixed = dot3(long, split(stacked), ((1,), (0,)))
    rows = []
    for k in range(4):
        re = mixed[:PEERS, LANES * k : LANES * (k + 1)]
        im = mixed[PEERS:, LANES * k : LANES * (k + 1)]
        rows.append(jnp.concatenate(twist(re, im, turn_cos, turn_sin), axis=1))
    return dot3(split(jnp.concatenate(rows, axis=0)), short, ((1,), (0,)))


def column_inverse(real, imag, turn_cos, turn_sin, long, short):
    mixed = dot3(split(jnp.concatenate([real, imag], axis=1)), short, ((1,), (0,)))
    first, second = [], []
    for k in range(4):
        block = mixed[PEERS * k : PEERS * (k + 1)]
        re, im = twist(block[:, :LANES], block[:, LANES:], turn_cos, turn_sin)
        first.append(re)
        second.append(im)
    stacked = jnp.concatenate(
        [jnp.concatenate(first, axis=1), jnp.concatenate(second, axis=1)], axis=0
    )
    return dot3(long, split(stacked), ((1,), (0,)))


def filter_block(owner, k2lo, led):
    lane = lax.broadcasted_iota(jnp.int32, (PEERS, LANES), 1)
    v1 = lax.broadcasted_iota(jnp.int32, (PEERS, LANES), 0)
    u = (lane >> 4) + 8 * (OWNERS * k2lo + owner)
    v = v1 + PEERS * (lane & (ROWS - 1))
    kx = (led // GRID - GRID // 2) * SHIFT
    ky = (led % GRID - GRID // 2) * SHIFT
    fx = (((u + N // 2) & (N - 1)) - N // 2 + kx).astype(F32) * (1.0 / N)
    fy = (((v + N // 2) & (N - 1)) - N // 2 + ky).astype(F32) * (1.0 / N)
    turns = DZ * (jnp.sqrt(1.0 - fx * fx - fy * fy) - 1.0)
    cosine, sine = cos_sin_turns(turns)
    return cosine * (1.0 / (N * N)), sine * (1.0 / (N * N))


def kernel(
    led_hbm, fields_hbm, phases_hbm, residual_hbm, wide_hbm, long_hbm, short_hbm, trow_hbm, tcol_hbm,
    slopes, wave,
    led_ref, fields, phases, wide_f32, long_f32, short_f32, trow, tcol, wide_ref, long_ref, short_ref,
    filt, trans, col_out, col_in, row_out, row_in, slope_out, slope_in,
    load_sem, col_send_sem, col_recv_sem, row_send_sem, row_recv_sem, lsend_sem, lrecv_sem,
):
    me = lax.axis_index("row")
    group = lax.axis_index("led")
    my_y, my_w = me // 8, me % 8
    my_x, my_z = my_w // 2, my_w % 2
    my_led = lax.rem(my_x + my_y, 2)
    my_owner = my_y * 4 + my_x // 2 * 2 + my_z
    led_peers = [lax.rem(group + d, GROUPS) for d in (4, 3, 5, 2, 6, 7, 1)]

    loads = [
        pltpu.make_async_copy(src, dst, load_sem.at[n])
        for n, (src, dst) in enumerate(
            [
                (residual_hbm, wave),
                (trow_hbm, trow),
                (wide_hbm, wide_f32),
                (tcol_hbm, tcol),
                (long_hbm, long_f32),
                (short_hbm, short_f32),
                (phases_hbm, phases),
                (fields_hbm, fields),
                (led_hbm, led_ref),
            ]
        )
    ]
    for load in loads:
        load.start()

    barrier = pltpu.get_barrier_semaphore()

    @pl.loop(1, PEERS)
    def _(step):
        peer = lax.rem(me + step, PEERS)
        pl.semaphore_signal(barrier, inc=1, device_id=(group, peer), device_id_type=MESH)

    for peer in led_peers:
        pl.semaphore_signal(barrier, inc=1, device_id=(peer, me), device_id_type=MESH)

    for load in loads[:3]:
        load.wait()
    turn_cos = [trow[k : k + 1, :] for k in range(8)]
    turn_sin = [trow[8 + k : 9 + k, :] for k in range(8)]
    wide_ref[0], wide_ref[1] = split(wide_f32[...])

    def halves(table):
        return table[0], table[1]

    near_far = (4, 3, 5, 2, 6, 1, 7, 0)

    def copy_tile(source, target, send_sem, recv_sem, peer):
        pltpu.make_async_remote_copy(
            src_ref=source,
            dst_ref=target,
            send_sem=send_sem,
            recv_sem=recv_sem,
            device_id=(group, peer),
            device_id_type=MESH,
        ).start()

    def send_columns(turn, led):
        target = col_in.at[turn, me]
        sem = col_recv_sem.at[turn]

        def to(dy, dx, dz):
            y, half, z = lax.rem(my_y + dy, 8), lax.rem(my_x // 2 + dx, 2), lax.rem(my_z + dz, 2)
            source = col_out.at[turn, led, y * 4 + half * 2 + z]
            return source, y * 8 + half * 4 + lax.rem(led + y, 2) * 2 + z

        for dx, dz in ((1, 1), (1, 0), (0, 1), (0, 0)):
            for dy in near_far:
                if dy + dx + dz > 0:
                    source, peer = to(dy, dx, dz)
                    copy_tile(source, target, col_send_sem.at[turn], sem, peer)
        source, peer = to(0, 0, 0)

        @pl.when(led == my_led)
        def _():
            pltpu.make_async_copy(source, target, sem).start()

        @pl.when(led != my_led)
        def _():
            copy_tile(source, target, col_send_sem.at[turn], sem, peer)

    def send_rows(turn):
        target = row_in.at[turn, my_led, my_owner]
        sem = row_recv_sem.at[turn, my_led]
        for dw in (5, 4, 3, 1, 7, 2, 6, 0):
            for dy in near_far:
                if dw + dy > 0:
                    peer = lax.rem(my_y + dy, 8) * 8 + lax.rem(my_w + dw, 8)
                    copy_tile(row_out.at[turn, peer], target, row_send_sem.at[turn], sem, peer)
        pltpu.make_async_copy(row_out.at[turn, me], target, sem).start()

    def put(values, box, peers):
        flat = box.reshape(peers * TILE, LANES)
        for j in range(TILE):
            flat[pl.ds(j, peers, stride=TILE), :] = values[j]

    def arrived(box, sem, peers):
        pltpu.make_async_copy(box, box, sem).wait()
        flat = box.reshape(peers * TILE, LANES)
        return [flat[pl.ds(j, peers, stride=TILE), :] for j in range(TILE)]

    def columns_of(ref, c):
        return [ref[c, :, LANES * a : LANES * (a + 1)] for a in range(8)]

    def to_columns(turn, led):
        seed = wave.at[led]
        spectrum = row_forward(
            columns_of(seed, 0), columns_of(seed, 1), turn_cos, turn_sin, halves(wide_ref)
        )
        values = [spectrum[OWNERS * j : OWNERS * (j + 1)] for j in range(TILE)]
        put(values, col_out.at[turn, led], OWNERS)

    def column_pass(turn):
        tiles = arrived(col_in.at[turn], col_recv_sem.at[turn], PEERS)
        spectrum = column_forward([tiles[:4], tiles[4:]], tcol[0], tcol[1], halves(long_ref), halves(short_ref))
        real, imag = twist(spectrum[:, :LANES], spectrum[:, LANES:], filt[0], filt[1])
        back = column_inverse(imag, real, tcol[0], tcol[1], halves(long_ref), halves(short_ref))
        values = [
            back[PEERS * (1 - c) : PEERS * (2 - c), LANES * k : LANES * (k + 1)]
            for c in range(2)
            for k in range(4)
        ]
        put(values, row_out.at[turn], PEERS)
        send_rows(turn)

    def send_slopes(turn):
        for peer in led_peers:
            pltpu.make_async_remote_copy(
                src_ref=slope_out.at[turn, peer],
                dst_ref=slope_in.at[turn, group],
                send_sem=lsend_sem.at[turn],
                recv_sem=lrecv_sem.at[turn],
                device_id=(peer, me),
                device_id_type=MESH,
            ).start()
        pltpu.make_async_copy(
            slope_out.at[turn, group], slope_in.at[turn, group], lrecv_sem.at[turn]
        ).start()

    def from_columns(turn, led):
        layer = SLICES - 1 - turn
        tiles = arrived(row_in.at[turn, led], row_recv_sem.at[turn, led], OWNERS)
        swapped = jnp.concatenate(tiles[4:] + tiles[:4], axis=0)
        imag, real = row_inverse(swapped, turn_cos, turn_sin, halves(wide_ref))
        for a in range(8):
            cols = slice(LANES * a, LANES * (a + 1))
            re, im = twist(real[a], imag[a], trans[layer, 0, :, cols], trans[layer, 1, :, cols])
            wave[led, 0, :, cols] = re
            wave[led, 1, :, cols] = im

    def slope_terms(turn, led):
        layer = SLICES - 1 - turn
        for a in range(8):
            cols = slice(LANES * a, LANES * (a + 1))
            slope_out[turn, a] += (
                fields[layer, led, 0, :, cols] * wave[led, 1, :, cols]
                - fields[layer, led, 1, :, cols] * wave[led, 0, :, cols]
            )

    slope_out[...] = jnp.zeros_like(slope_out)

    @pl.loop(0, SLICES + 1)
    def _(phase):
        @pl.loop(0, LEDS)
        def _(led):
            @pl.when(phase > 0)
            def _():
                from_columns(phase - 1, led)

            @pl.when(phase < SLICES)
            def _():
                to_columns(phase, led)

                @pl.when(phase + led == 0)
                def _():
                    pl.semaphore_wait(barrier, PEERS - 1 + GROUPS - 1)

                send_columns(phase, led)

            @pl.when(phase > 0)
            def _():
                slope_terms(phase - 1, led)

                @pl.when(led == LEDS - 1)
                def _():
                    send_slopes(phase - 1)

        @pl.when(phase == 0)
        def _():
            for load in loads[3:]:
                load.wait()
            for k in range(4):
                cosine, sine = filter_block(my_owner, k, led_ref[my_led])
                filt[0, PEERS * k : PEERS * (k + 1), :] = cosine
                filt[1, PEERS * k : PEERS * (k + 1), :] = sine
            long_ref[0], long_ref[1] = split(long_f32[...])
            short_ref[0], short_ref[1] = split(short_f32[...])
            for layer in range(SLICES):
                cosine, sine = cos_sin_turns(phases[layer] * (0.5 / math.pi))
                trans[layer, 0] = cosine
                trans[layer, 1] = sine

        @pl.when(phase < SLICES)
        def _():
            column_pass(phase)

    for turn in range(SLICES):
        pltpu.make_async_copy(slope_in.at[turn], slope_in.at[turn], lrecv_sem.at[turn]).wait()
        slopes[SLICES - 1 - turn] = jnp.sum(slope_in[turn], axis=0) * (1.0 / (LEDS * GROUPS))
    for turn in range(SLICES):
        sent = row_out.at[turn, pl.ds(0, PEERS - 1)]
        for sem in (row_send_sem, col_send_sem):
            pltpu.make_async_copy(sent, sent, sem.at[turn]).wait()
    for turn in range(SLICES):
        sent = slope_out.at[turn, pl.ds(0, GROUPS - 1)]
        pltpu.make_async_copy(sent, sent, lsend_sem.at[turn]).wait()


def local(fields, phases, residual, led_index):
    consts = [jnp.asarray(t) for t in tables()]
    scratch = [
        pltpu.SMEM(led_index.shape, jnp.int32),
        pltpu.VMEM(fields.shape, F32),
        pltpu.VMEM(phases.shape, F32),
    ]
    scratch += [pltpu.VMEM(t.shape, t.dtype) for t in consts]
    scratch += [pltpu.VMEM((2,) + t.shape, BF16) for t in consts[:3]]
    scratch += [
        pltpu.VMEM((2, 4 * PEERS, LANES), F32),
        pltpu.VMEM((SLICES, 2, ROWS, N), F32),
    ]
    to_col = pltpu.VMEM((SLICES, LEDS, OWNERS, TILE, LANES), F32)
    to_row = pltpu.VMEM((SLICES, PEERS, TILE, LANES), F32)
    scratch += [to_col, to_row, to_row, to_col]
    scratch += [
        pltpu.VMEM((SLICES, GROUPS, ROWS, LANES), F32),
        pltpu.VMEM((SLICES, GROUPS, ROWS, LANES), F32),
        pltpu.SemaphoreType.DMA((9,)),
        pltpu.SemaphoreType.DMA((SLICES,)),
        pltpu.SemaphoreType.DMA((SLICES,)),
        pltpu.SemaphoreType.DMA((SLICES,)),
        pltpu.SemaphoreType.DMA((SLICES, LEDS)),
        pltpu.SemaphoreType.DMA((SLICES,)),
        pltpu.SemaphoreType.DMA((SLICES,)),
    ]
    held = [
        pltpu.with_memory_space_constraint(x, pltpu.HBM) for x in [led_index, fields, phases, residual] + consts
    ]
    anywhere = pl.BlockSpec(memory_space=pl.ANY)
    return pl.pallas_call(
        kernel,
        out_shape=(
            pltpu.VMEM((SLICES, ROWS, LANES), F32),
            pltpu.VMEM(residual.shape, F32),
        ),
        in_specs=[anywhere] * 9,
        out_specs=(pl.BlockSpec(memory_space=pltpu.VMEM),) * 2,
        scratch_shapes=scratch,
        compiler_params=pltpu.CompilerParams(
            collective_id=0, has_side_effects=True, vmem_limit_bytes=VMEM_LIMIT
        ),
        name="adjoint",
    )(*held)


def solution(mesh):
    in_specs = (
        P(None, "led", None, "row", None),
        P(None, "row", None),
        P("led", None, "row", None),
        P("led"),
    )
    out_specs = (P(None, "row", "led"), P("led", None, "row", None))
    return jax.shard_map(local, mesh=mesh, in_specs=in_specs, out_specs=out_specs, check_vma=False)
```

```python
import math

import jax
import jax.numpy as jnp
import numpy as np
from jax import lax
from jax.experimental import pallas as pl
from jax.experimental.pallas import tpu as pltpu
from jax.sharding import PartitionSpec as P

N = 1024
GRID = 15
DZ = 64
SHIFT = 10
LANES = 128
VMEM_LIMIT = 40 * 1024 * 1024
ROWS = 16
PEERS = 64
OWNERS = 32
HALVES = 2
PART = 4
GROUPS = 8
LEDS = 2
SLICES = 2
MESH = pl.DeviceIdType.MESH
F32 = jnp.float32
BF16 = jnp.bfloat16


def dft_block(length):
    index = np.arange(length)
    angle = 2.0 * np.pi * (np.outer(index, index) % length) / length
    return np.cos(angle), np.sin(angle)


def complex_left(length):
    cos, sin = dft_block(length)
    return np.block([[cos, sin], [-sin, cos]])


def tables():
    wide = complex_left(LANES).astype(np.float32)
    long = complex_left(PEERS).astype(np.float32)
    cos, sin = dft_block(ROWS)
    eye = np.eye(LANES // ROWS)
    cos, sin = np.kron(eye, cos), np.kron(eye, sin)
    short = np.block([[cos, -sin], [sin, cos]]).astype(np.float32)
    angle = 2.0 * np.pi * np.outer(np.arange(8), np.arange(LANES)) / N
    turn_rows = np.concatenate([np.cos(angle), np.sin(angle)]).astype(np.float32)
    angle = 2.0 * np.pi * np.outer(np.arange(PEERS), np.arange(LANES) % ROWS) / N
    turn_cols = np.stack([np.cos(angle), np.sin(angle)]).astype(np.float32)
    return wide, long, short, turn_rows, turn_cols


def fit_turns():
    nodes = 0.5 * np.cos(np.pi * (np.arange(400) + 0.5) / 800)
    square = nodes * nodes
    basis = np.vander(square, 8, increasing=True)
    sin_fit = np.linalg.lstsq(basis, np.sin(2 * np.pi * nodes) / nodes, rcond=None)[0]
    cos_fit = np.linalg.lstsq(basis, np.cos(2 * np.pi * nodes), rcond=None)[0]
    return [float(v) for v in sin_fit], [float(v) for v in cos_fit]


SIN_FIT, COS_FIT = fit_turns()


def cos_sin_turns(turns):
    frac = turns - jnp.floor(turns + 0.5)
    square = frac * frac
    sine = jnp.full_like(square, SIN_FIT[-1])
    cosine = jnp.full_like(square, COS_FIT[-1])
    for s, c in zip(SIN_FIT[-2::-1], COS_FIT[-2::-1]):
        sine = sine * square + s
        cosine = cosine * square + c
    return cosine, sine * frac


def split(value):
    high = value.astype(BF16)
    return high, (value - high.astype(F32)).astype(BF16)


def dot3(left, right, dims):
    def dot(a, b):
        return lax.dot_general(a, b, (dims, ((), ())), preferred_element_type=F32)

    return dot(left[0], right[0]) + (dot(left[0], right[1]) + dot(left[1], right[0]))


def radix8(real, imag):
    half = math.sqrt(0.5)

    def pair(a, b):
        return (a[0] + b[0], a[1] + b[1]), (a[0] - b[0], a[1] - b[1])

    def minus_i(a):
        return a[1], -a[0]

    def four(z):
        s0, d0 = pair(z[0], z[2])
        s1, d1 = pair(z[1], z[3])
        y0, y2 = pair(s0, s1)
        y1, y3 = pair(d0, minus_i(d1))
        return [y0, y1, y2, y3]

    z = list(zip(real, imag))
    even = four([z[0], z[2], z[4], z[6]])
    odd = four([z[1], z[3], z[5], z[7]])
    odd[1] = ((odd[1][0] + odd[1][1]) * half, (odd[1][1] - odd[1][0]) * half)
    odd[2] = minus_i(odd[2])
    odd[3] = ((odd[3][1] - odd[3][0]) * half, (odd[3][0] + odd[3][1]) * -half)
    out = [None] * 8
    for k in range(4):
        out[k], out[k + 4] = pair(even[k], odd[k])
    return [o[0] for o in out], [o[1] for o in out]


def twist(real, imag, cos, sin):
    return real * cos + imag * sin, imag * cos - real * sin


def row_forward(real, imag, turn_cos, turn_sin, wide):
    real, imag = radix8(real, imag)
    rows = []
    for k in range(8):
        re, im = (real[k], imag[k]) if k == 0 else twist(real[k], imag[k], turn_cos[k], turn_sin[k])
        rows.append(jnp.concatenate([re, im], axis=1))
    return dot3(wide, split(jnp.concatenate(rows, axis=0)), ((1,), (1,)))


def row_inverse(swapped, turn_cos, turn_sin, wide):
    spread = dot3(wide, split(swapped), ((1,), (0,)))
    first = spread[:LANES].T
    second = spread[LANES:].T
    real, imag = [], []
    for k in range(8):
        re, im = first[ROWS * k : ROWS * (k + 1)], second[ROWS * k : ROWS * (k + 1)]
        if k > 0:
            re, im = twist(re, im, turn_cos[k], turn_sin[k])
        real.append(re)
        imag.append(im)
    return radix8(real, imag)


def column_forward(blocks, turn_cos, turn_sin, long, short):
    stacked = jnp.concatenate([jnp.concatenate(blocks[c], axis=1) for c in range(2)], axis=0)
    mixed = dot3(long, split(stacked), ((1,), (0,)))
    rows = []
    for k in range(2):
        re = mixed[:PEERS, LANES * k : LANES * (k + 1)]
        im = mixed[PEERS:, LANES * k : LANES * (k + 1)]
        rows.append(jnp.concatenate(twist(re, im, turn_cos, turn_sin), axis=1))
    return dot3(split(jnp.concatenate(rows, axis=0)), short, ((1,), (0,)))


def column_inverse(real, imag, turn_cos, turn_sin, long, short):
    mixed = dot3(split(jnp.concatenate([real, imag], axis=1)), short, ((1,), (0,)))
    first, second = [], []
    for k in range(2):
        block = mixed[PEERS * k : PEERS * (k + 1)]
        re, im = twist(block[:, :LANES], block[:, LANES:], turn_cos, turn_sin)
        first.append(re)
        second.append(im)
    stacked = jnp.concatenate(
        [jnp.concatenate(first, axis=1), jnp.concatenate(second, axis=1)], axis=0
    )
    return dot3(long, split(stacked), ((1,), (0,)))


def filter_block(owner, k2lo, led):
    lane = lax.broadcasted_iota(jnp.int32, (PEERS, LANES), 1)
    v1 = lax.broadcasted_iota(jnp.int32, (PEERS, LANES), 0)
    u = (lane >> 4) + 8 * (OWNERS * k2lo + owner)
    v = v1 + PEERS * (lane & (ROWS - 1))
    kx = (led // GRID - GRID // 2) * SHIFT
    ky = (led % GRID - GRID // 2) * SHIFT
    fx = (((u + N // 2) & (N - 1)) - N // 2 + kx).astype(F32) * (1.0 / N)
    fy = (((v + N // 2) & (N - 1)) - N // 2 + ky).astype(F32) * (1.0 / N)
    turns = DZ * (jnp.sqrt(1.0 - fx * fx - fy * fy) - 1.0)
    cosine, sine = cos_sin_turns(turns)
    return cosine * (1.0 / (N * N)), sine * (1.0 / (N * N))


def kernel(
    led_hbm, fields_hbm, phases_hbm, residual_hbm, wide_hbm, long_hbm, short_hbm, trow_hbm, tcol_hbm,
    slopes, wave,
    led_ref, fields, phases, wide_f32, long_f32, short_f32, trow, tcol, wide_ref, long_ref, short_ref,
    filt, trans, col_out, col_in, row_out, row_in, slope_out, slope_in,
    load_sem, col_send_sem, col_recv_sem, row_send_sem, row_recv_sem, lsend_sem, lrecv_sem,
):
    me = lax.axis_index("row")
    group = lax.axis_index("led")
    my_y, my_w = me // 8, me % 8
    my_x, my_z = my_w // 2, my_w % 2
    my_led = lax.rem(my_x + my_y, 2)
    my_owner = my_y * 4 + my_x // 2 * 2 + my_z
    led_peers = [lax.rem(group + d, GROUPS) for d in (4, 3, 5, 2, 6, 7, 1)]

    loads = [
        pltpu.make_async_copy(src, dst, load_sem.at[n])
        for n, (src, dst) in enumerate(
            [
                (residual_hbm, wave),
                (trow_hbm, trow),
                (wide_hbm, wide_f32),
                (tcol_hbm, tcol),
                (long_hbm, long_f32),
                (short_hbm, short_f32),
                (phases_hbm, phases),
                (fields_hbm, fields),
                (led_hbm, led_ref),
            ]
        )
    ]
    for load in loads:
        load.start()

    barrier = pltpu.get_barrier_semaphore()

    @pl.loop(1, PEERS)
    def _(step):
        peer = lax.rem(me + step, PEERS)
        pl.semaphore_signal(barrier, inc=1, device_id=(group, peer), device_id_type=MESH)

    for peer in led_peers:
        pl.semaphore_signal(barrier, inc=1, device_id=(peer, me), device_id_type=MESH)

    for load in loads[:3]:
        load.wait()
    turn_cos = [trow[k : k + 1, :] for k in range(8)]
    turn_sin = [trow[8 + k : 9 + k, :] for k in range(8)]
    wide_ref[0], wide_ref[1] = split(wide_f32[...])

    def halves(table):
        return table[0], table[1]

    def away(step, ring):
        return min(step, ring - step)

    owner_steps = sorted(
        [(dy, dx, dz) for dy in (4, 3, 5, 2, 6, 1, 7, 0) for dx in (1, 0) for dz in (1, 0)],
        key=lambda step: -(away(step[0], 8) + 1.5 * step[1] + step[2]),
    )[:-1]
    row_steps = sorted(
        [(dy, dx, dz) for dy in (4, 3, 5, 2, 6, 1, 7, 0) for dx in (2, 1, 3, 0) for dz in (1, 0)],
        key=lambda step: -(away(step[0], 8) + away(step[1], 4) + step[2]),
    )[:-1]

    def copy_tile(source, target, send_sem, recv_sem, peer):
        pltpu.make_async_remote_copy(
            src_ref=source,
            dst_ref=target,
            send_sem=send_sem,
            recv_sem=recv_sem,
            device_id=(group, peer),
            device_id_type=MESH,
        ).start()

    def send_columns(turn, led, half):
        target = col_in.at[turn, half, me]
        sem = col_recv_sem.at[turn, half]
        sent = col_send_sem.at[turn, half]

        def to(dy, dx, dz):
            y, pair, z = lax.rem(my_y + dy, 8), lax.rem(my_x // 2 + dx, 2), lax.rem(my_z + dz, 2)
            source = col_out.at[turn, half, led, y * 4 + pair * 2 + z]
            return source, y * 8 + pair * 4 + lax.rem(led + y, 2) * 2 + z

        for step in owner_steps:
            source, peer = to(*step)
            copy_tile(source, target, sent, sem, peer)
        source, peer = to(0, 0, 0)

        @pl.when(led == my_led)
        def _():
            pltpu.make_async_copy(source, target, sem).start()

        @pl.when(led != my_led)
        def _():
            copy_tile(source, target, sent, sem, peer)

    def send_rows(turn, half):
        target = row_in.at[turn, half, my_led, my_owner]
        sem = row_recv_sem.at[turn, half, my_led]
        for dy, dx, dz in row_steps:
            y, x, z = lax.rem(my_y + dy, 8), lax.rem(my_x + dx, 4), lax.rem(my_z + dz, 2)
            peer = y * 8 + x * 2 + z
            copy_tile(row_out.at[turn, half, peer], target, row_send_sem.at[turn, half], sem, peer)
        pltpu.make_async_copy(row_out.at[turn, half, me], target, sem).start()

    def put(values, box, peers):
        flat = box.reshape(peers * PART, LANES)
        for j in range(PART):
            flat[pl.ds(j, peers, stride=PART), :] = values[j]

    def arrived(box, sem, peers):
        pltpu.make_async_copy(box, box, sem).wait()
        flat = box.reshape(peers * PART, LANES)
        return [flat[pl.ds(j, peers, stride=PART), :] for j in range(PART)]

    def columns_of(ref, c):
        return [ref[c, :, LANES * a : LANES * (a + 1)] for a in range(8)]

    def to_columns(turn, led):
        seed = wave.at[led]
        spectrum = row_forward(
            columns_of(seed, 0), columns_of(seed, 1), turn_cos, turn_sin, halves(wide_ref)
        )
        values = [spectrum[OWNERS * j : OWNERS * (j + 1)] for j in range(2 * PART)]
        put(values[0:2] + values[4:6], col_out.at[turn, 0, led], OWNERS)
        put(values[2:4] + values[6:8], col_out.at[turn, 1, led], OWNERS)

    def column_pass(turn, half):
        tiles = arrived(col_in.at[turn, half], col_recv_sem.at[turn, half], PEERS)
        spectrum = column_forward([tiles[:2], tiles[2:]], tcol[0], tcol[1], halves(long_ref), halves(short_ref))
        real, imag = twist(spectrum[:, :LANES], spectrum[:, LANES:], filt[half, 0], filt[half, 1])
        back = column_inverse(imag, real, tcol[0], tcol[1], halves(long_ref), halves(short_ref))
        values = [
            back[PEERS * (1 - c) : PEERS * (2 - c), LANES * k : LANES * (k + 1)]
            for c in range(2)
            for k in range(2)
        ]
        put(values, row_out.at[turn, half], PEERS)
        send_rows(turn, half)

    def send_slopes(turn):
        for peer in led_peers:
            pltpu.make_async_remote_copy(
                src_ref=slope_out.at[turn, peer],
                dst_ref=slope_in.at[turn, group],
                send_sem=lsend_sem.at[turn],
                recv_sem=lrecv_sem.at[turn],
                device_id=(peer, me),
                device_id_type=MESH,
            ).start()
        pltpu.make_async_copy(
            slope_out.at[turn, group], slope_in.at[turn, group], lrecv_sem.at[turn]
        ).start()

    def from_columns(turn, led):
        layer = SLICES - 1 - turn
        first, second = [
            arrived(row_in.at[turn, half, led], row_recv_sem.at[turn, half, led], OWNERS)
            for half in range(HALVES)
        ]
        swapped = jnp.concatenate(first[2:] + second[2:] + first[:2] + second[:2], axis=0)
        imag, real = row_inverse(swapped, turn_cos, turn_sin, halves(wide_ref))
        for a in range(8):
            cols = slice(LANES * a, LANES * (a + 1))
            re, im = twist(real[a], imag[a], trans[layer, 0, :, cols], trans[layer, 1, :, cols])
            wave[led, 0, :, cols] = re
            wave[led, 1, :, cols] = im

    def slope_terms(turn, led):
        layer = SLICES - 1 - turn
        for a in range(8):
            cols = slice(LANES * a, LANES * (a + 1))
            slope_out[turn, a] += (
                fields[layer, led, 0, :, cols] * wave[led, 1, :, cols]
                - fields[layer, led, 1, :, cols] * wave[led, 0, :, cols]
            )

    slope_out[...] = jnp.zeros_like(slope_out)

    @pl.loop(0, SLICES + 1)
    def _(phase):
        @pl.loop(0, LEDS)
        def _(led):
            @pl.when(phase > 0)
            def _():
                from_columns(phase - 1, led)

            @pl.when(phase < SLICES)
            def _():
                to_columns(phase, led)

                @pl.when(phase + led == 0)
                def _():
                    pl.semaphore_wait(barrier, PEERS - 1 + GROUPS - 1)

                for half in range(HALVES):
                    send_columns(phase, led, half)

            @pl.when(phase > 0)
            def _():
                slope_terms(phase - 1, led)

                @pl.when(led == LEDS - 1)
                def _():
                    send_slopes(phase - 1)

        @pl.when(phase == 0)
        def _():
            for load in loads[3:]:
                load.wait()
            for k in range(4):
                cosine, sine = filter_block(my_owner, k, led_ref[my_led])
                filt[k // 2, 0, PEERS * (k % 2) : PEERS * (k % 2 + 1), :] = cosine
                filt[k // 2, 1, PEERS * (k % 2) : PEERS * (k % 2 + 1), :] = sine
            long_ref[0], long_ref[1] = split(long_f32[...])
            short_ref[0], short_ref[1] = split(short_f32[...])
            for layer in range(SLICES):
                cosine, sine = cos_sin_turns(phases[layer] * (0.5 / math.pi))
                trans[layer, 0] = cosine
                trans[layer, 1] = sine

        @pl.when(phase < SLICES)
        def _():
            @pl.loop(0, HALVES)
            def _(half):
                column_pass(phase, half)

    for turn in range(SLICES):
        pltpu.make_async_copy(slope_in.at[turn], slope_in.at[turn], lrecv_sem.at[turn]).wait()
        slopes[SLICES - 1 - turn] = jnp.sum(slope_in[turn], axis=0) * (1.0 / (LEDS * GROUPS))
    for turn in range(SLICES):
        for half in range(HALVES):
            sent = row_out.at[turn, half, pl.ds(0, PEERS - 1)]
            for sem in (row_send_sem, col_send_sem):
                pltpu.make_async_copy(sent, sent, sem.at[turn, half]).wait()
    for turn in range(SLICES):
        sent = slope_out.at[turn, pl.ds(0, GROUPS - 1)]
        pltpu.make_async_copy(sent, sent, lsend_sem.at[turn]).wait()


def local(fields, phases, residual, led_index):
    consts = [jnp.asarray(t) for t in tables()]
    scratch = [
        pltpu.SMEM(led_index.shape, jnp.int32),
        pltpu.VMEM(fields.shape, F32),
        pltpu.VMEM(phases.shape, F32),
    ]
    scratch += [pltpu.VMEM(t.shape, t.dtype) for t in consts]
    scratch += [pltpu.VMEM((2,) + t.shape, BF16) for t in consts[:3]]
    scratch += [
        pltpu.VMEM((HALVES, 2, 2 * PEERS, LANES), F32),
        pltpu.VMEM((SLICES, 2, ROWS, N), F32),
    ]
    to_col = pltpu.VMEM((SLICES, HALVES, LEDS, OWNERS, PART, LANES), F32)
    to_row = pltpu.VMEM((SLICES, HALVES, PEERS, PART, LANES), F32)
    scratch += [to_col, to_row, to_row, to_col]
    scratch += [
        pltpu.VMEM((SLICES, GROUPS, ROWS, LANES), F32),
        pltpu.VMEM((SLICES, GROUPS, ROWS, LANES), F32),
        pltpu.SemaphoreType.DMA((9,)),
        pltpu.SemaphoreType.DMA((SLICES, HALVES)),
        pltpu.SemaphoreType.DMA((SLICES, HALVES)),
        pltpu.SemaphoreType.DMA((SLICES, HALVES)),
        pltpu.SemaphoreType.DMA((SLICES, HALVES, LEDS)),
        pltpu.SemaphoreType.DMA((SLICES,)),
        pltpu.SemaphoreType.DMA((SLICES,)),
    ]
    held = [
        pltpu.with_memory_space_constraint(x, pltpu.HBM) for x in [led_index, fields, phases, residual] + consts
    ]
    anywhere = pl.BlockSpec(memory_space=pl.ANY)
    return pl.pallas_call(
        kernel,
        out_shape=(
            pltpu.VMEM((SLICES, ROWS, LANES), F32),
            pltpu.VMEM(residual.shape, F32),
        ),
        in_specs=[anywhere] * 9,
        out_specs=(pl.BlockSpec(memory_space=pltpu.VMEM),) * 2,
        scratch_shapes=scratch,
        compiler_params=pltpu.CompilerParams(
            collective_id=0, has_side_effects=True, vmem_limit_bytes=VMEM_LIMIT
        ),
        name="adjoint",
    )(*held)


def solution(mesh):
    in_specs = (
        P(None, "led", None, "row", None),
        P(None, "row", None),
        P("led", None, "row", None),
        P("led"),
    )
    out_specs = (P(None, "row", "led"), P("led", None, "row", None))
    return jax.shard_map(local, mesh=mesh, in_specs=in_specs, out_specs=out_specs, check_vma=False)
```

```python
import math

import jax
import jax.numpy as jnp
import numpy as np
from jax import lax
from jax.experimental import pallas as pl
from jax.experimental.pallas import tpu as pltpu
from jax.sharding import PartitionSpec as P

N = 1024
GRID = 15
DZ = 64
SHIFT = 10
LANES = 128
VMEM_LIMIT = 40 * 1024 * 1024
ROWS = 16
PEERS = 64
OWNERS = 32
HALVES = 2
PART = 4
GROUPS = 8
LEDS = 2
SLICES = 2
MESH = pl.DeviceIdType.MESH
F32 = jnp.float32
BF16 = jnp.bfloat16


def dft_block(length):
    index = np.arange(length)
    angle = 2.0 * np.pi * (np.outer(index, index) % length) / length
    return np.cos(angle), np.sin(angle)


def complex_left(length):
    cos, sin = dft_block(length)
    return np.block([[cos, sin], [-sin, cos]])


def tables():
    wide = complex_left(LANES).astype(np.float32)
    long = complex_left(PEERS).astype(np.float32)
    cos, sin = dft_block(ROWS)
    eye = np.eye(LANES // ROWS)
    cos, sin = np.kron(eye, cos), np.kron(eye, sin)
    short = np.block([[cos, -sin], [sin, cos]]).astype(np.float32)
    angle = 2.0 * np.pi * np.outer(np.arange(8), np.arange(LANES)) / N
    turn_rows = np.concatenate([np.cos(angle), np.sin(angle)]).astype(np.float32)
    angle = 2.0 * np.pi * np.outer(np.arange(PEERS), np.arange(LANES) % ROWS) / N
    turn_cols = np.stack([np.cos(angle), np.sin(angle)]).astype(np.float32)
    return wide, long, short, turn_rows, turn_cols


def fit_turns():
    nodes = 0.5 * np.cos(np.pi * (np.arange(400) + 0.5) / 800)
    square = nodes * nodes
    basis = np.vander(square, 8, increasing=True)
    sin_fit = np.linalg.lstsq(basis, np.sin(2 * np.pi * nodes) / nodes, rcond=None)[0]
    cos_fit = np.linalg.lstsq(basis, np.cos(2 * np.pi * nodes), rcond=None)[0]
    return [float(v) for v in sin_fit], [float(v) for v in cos_fit]


SIN_FIT, COS_FIT = fit_turns()


def cos_sin_turns(turns):
    frac = turns - jnp.floor(turns + 0.5)
    square = frac * frac
    sine = jnp.full_like(square, SIN_FIT[-1])
    cosine = jnp.full_like(square, COS_FIT[-1])
    for s, c in zip(SIN_FIT[-2::-1], COS_FIT[-2::-1]):
        sine = sine * square + s
        cosine = cosine * square + c
    return cosine, sine * frac


def split(value):
    high = value.astype(BF16)
    return high, (value - high.astype(F32)).astype(BF16)


def dot3(left, right, dims):
    def dot(a, b):
        return lax.dot_general(a, b, (dims, ((), ())), preferred_element_type=F32)

    return dot(left[0], right[0]) + (dot(left[0], right[1]) + dot(left[1], right[0]))


def radix8(real, imag):
    half = math.sqrt(0.5)

    def pair(a, b):
        return (a[0] + b[0], a[1] + b[1]), (a[0] - b[0], a[1] - b[1])

    def minus_i(a):
        return a[1], -a[0]

    def four(z):
        s0, d0 = pair(z[0], z[2])
        s1, d1 = pair(z[1], z[3])
        y0, y2 = pair(s0, s1)
        y1, y3 = pair(d0, minus_i(d1))
        return [y0, y1, y2, y3]

    z = list(zip(real, imag))
    even = four([z[0], z[2], z[4], z[6]])
    odd = four([z[1], z[3], z[5], z[7]])
    odd[1] = ((odd[1][0] + odd[1][1]) * half, (odd[1][1] - odd[1][0]) * half)
    odd[2] = minus_i(odd[2])
    odd[3] = ((odd[3][1] - odd[3][0]) * half, (odd[3][0] + odd[3][1]) * -half)
    out = [None] * 8
    for k in range(4):
        out[k], out[k + 4] = pair(even[k], odd[k])
    return [o[0] for o in out], [o[1] for o in out]


def twist(real, imag, cos, sin):
    return real * cos + imag * sin, imag * cos - real * sin


def row_forward(real, imag, turn_cos, turn_sin, wide):
    real, imag = radix8(real, imag)
    rows = []
    for k in range(8):
        re, im = (real[k], imag[k]) if k == 0 else twist(real[k], imag[k], turn_cos[k], turn_sin[k])
        rows.append(jnp.concatenate([re, im], axis=1))
    return dot3(wide, split(jnp.concatenate(rows, axis=0)), ((1,), (1,)))


def row_inverse(swapped, turn_cos, turn_sin, wide):
    spread = dot3(wide, split(swapped), ((1,), (0,)))
    first = spread[:LANES].T
    second = spread[LANES:].T
    real, imag = [], []
    for k in range(8):
        re, im = first[ROWS * k : ROWS * (k + 1)], second[ROWS * k : ROWS * (k + 1)]
        if k > 0:
            re, im = twist(re, im, turn_cos[k], turn_sin[k])
        real.append(re)
        imag.append(im)
    return radix8(real, imag)


def column_forward(blocks, turn_cos, turn_sin, long, short):
    stacked = jnp.concatenate([jnp.concatenate(blocks[c], axis=1) for c in range(2)], axis=0)
    mixed = dot3(long, split(stacked), ((1,), (0,)))
    rows = []
    for k in range(2):
        re = mixed[:PEERS, LANES * k : LANES * (k + 1)]
        im = mixed[PEERS:, LANES * k : LANES * (k + 1)]
        rows.append(jnp.concatenate(twist(re, im, turn_cos, turn_sin), axis=1))
    return dot3(split(jnp.concatenate(rows, axis=0)), short, ((1,), (0,)))


def column_inverse(real, imag, turn_cos, turn_sin, long, short):
    mixed = dot3(split(jnp.concatenate([real, imag], axis=1)), short, ((1,), (0,)))
    first, second = [], []
    for k in range(2):
        block = mixed[PEERS * k : PEERS * (k + 1)]
        re, im = twist(block[:, :LANES], block[:, LANES:], turn_cos, turn_sin)
        first.append(re)
        second.append(im)
    stacked = jnp.concatenate(
        [jnp.concatenate(first, axis=1), jnp.concatenate(second, axis=1)], axis=0
    )
    return dot3(long, split(stacked), ((1,), (0,)))


def filter_block(owner, k2lo, led):
    lane = lax.broadcasted_iota(jnp.int32, (PEERS, LANES), 1)
    v1 = lax.broadcasted_iota(jnp.int32, (PEERS, LANES), 0)
    u = (lane >> 4) + 8 * (OWNERS * k2lo + owner)
    v = v1 + PEERS * (lane & (ROWS - 1))
    kx = (led // GRID - GRID // 2) * SHIFT
    ky = (led % GRID - GRID // 2) * SHIFT
    fx = (((u + N // 2) & (N - 1)) - N // 2 + kx).astype(F32) * (1.0 / N)
    fy = (((v + N // 2) & (N - 1)) - N // 2 + ky).astype(F32) * (1.0 / N)
    turns = DZ * (jnp.sqrt(1.0 - fx * fx - fy * fy) - 1.0)
    cosine, sine = cos_sin_turns(turns)
    return cosine * (1.0 / (N * N)), sine * (1.0 / (N * N))


def kernel(
    led_hbm, fields_hbm, phases_hbm, residual_hbm, wide_hbm, long_hbm, short_hbm, trow_hbm, tcol_hbm,
    slopes, wave,
    led_ref, fields, phases, wide_f32, long_f32, short_f32, trow, tcol, wide_ref, long_ref, short_ref,
    filt, trans, col_out, col_in, row_out, row_in, slope_out, slope_in,
    ready_sem, load_sem, col_send_sem, col_recv_sem, row_send_sem, row_recv_sem, lsend_sem, lrecv_sem,
):
    me = lax.axis_index("row")
    group = lax.axis_index("led")
    my_y, my_w = me // 8, me % 8
    my_x, my_z = my_w // 2, my_w % 2
    my_led = lax.rem(my_x + my_y, 2)
    my_owner = my_y * 4 + my_x // 2 * 2 + my_z
    led_peers = [lax.rem(group + d, GROUPS) for d in (4, 3, 5, 2, 6, 7, 1)]

    loads = [
        pltpu.make_async_copy(src, dst, load_sem.at[n])
        for n, (src, dst) in enumerate(
            [
                (residual_hbm, wave),
                (trow_hbm, trow),
                (wide_hbm, wide_f32),
                (tcol_hbm, tcol),
                (long_hbm, long_f32),
                (short_hbm, short_f32),
                (phases_hbm, phases),
                (fields_hbm, fields),
                (led_hbm, led_ref),
            ]
        )
    ]
    for load in loads:
        load.start()

    barrier = pltpu.get_barrier_semaphore()

    w_peers = [my_y * 8 + lax.rem(my_w + d, 8) for d in range(1, 8)]
    y_peers = [lax.rem(my_y + d, 8) * 8 + my_w for d in range(1, 8)]
    for peer in y_peers + w_peers:
        pl.semaphore_signal(barrier, inc=1, device_id=(group, peer), device_id_type=MESH)
    for peer in led_peers:
        pl.semaphore_signal(barrier, inc=1, device_id=(peer, me), device_id_type=MESH)
    pl.semaphore_wait(barrier, 21)
    for peer in w_peers:
        pl.semaphore_signal(ready_sem, inc=1, device_id=(group, peer), device_id_type=MESH)

    for load in loads[:3]:
        load.wait()
    turn_cos = [trow[k : k + 1, :] for k in range(8)]
    turn_sin = [trow[8 + k : 9 + k, :] for k in range(8)]
    wide_ref[0], wide_ref[1] = split(wide_f32[...])

    def halves(table):
        return table[0], table[1]

    def away(step, ring):
        return min(step, ring - step)

    owner_steps = sorted(
        [(dy, dx, dz) for dy in (4, 3, 5, 2, 6, 1, 7, 0) for dx in (1, 0) for dz in (1, 0)],
        key=lambda step: -(away(step[0], 8) + 1.5 * step[1] + step[2]),
    )[:-1]
    row_steps = sorted(
        [(dy, dx, dz) for dy in (4, 3, 5, 2, 6, 1, 7, 0) for dx in (2, 1, 3, 0) for dz in (1, 0)],
        key=lambda step: -(away(step[0], 8) + away(step[1], 4) + step[2]),
    )[:-1]

    def copy_tile(source, target, send_sem, recv_sem, peer):
        pltpu.make_async_remote_copy(
            src_ref=source,
            dst_ref=target,
            send_sem=send_sem,
            recv_sem=recv_sem,
            device_id=(group, peer),
            device_id_type=MESH,
        ).start()

    def send_columns(turn, led, half):
        target = col_in.at[turn, half, me]
        sem = col_recv_sem.at[turn, half]
        sent = col_send_sem.at[turn, half]

        def to(dy, dx, dz):
            y, pair, z = lax.rem(my_y + dy, 8), lax.rem(my_x // 2 + dx, 2), lax.rem(my_z + dz, 2)
            source = col_out.at[turn, half, led, y * 4 + pair * 2 + z]
            return source, y * 8 + pair * 4 + lax.rem(led + y, 2) * 2 + z

        for step in owner_steps:
            source, peer = to(*step)
            copy_tile(source, target, sent, sem, peer)
        source, peer = to(0, 0, 0)

        @pl.when(led == my_led)
        def _():
            pltpu.make_async_copy(source, target, sem).start()

        @pl.when(led != my_led)
        def _():
            copy_tile(source, target, sent, sem, peer)

    def send_rows(turn, half):
        target = row_in.at[turn, half, my_led, my_owner]
        sem = row_recv_sem.at[turn, half, my_led]
        for dy, dx, dz in row_steps:
            y, x, z = lax.rem(my_y + dy, 8), lax.rem(my_x + dx, 4), lax.rem(my_z + dz, 2)
            peer = y * 8 + x * 2 + z
            copy_tile(row_out.at[turn, half, peer], target, row_send_sem.at[turn, half], sem, peer)
        pltpu.make_async_copy(row_out.at[turn, half, me], target, sem).start()

    def put(values, box, peers):
        flat = box.reshape(peers * PART, LANES)
        for j in range(PART):
            flat[pl.ds(j, peers, stride=PART), :] = values[j]

    def arrived(box, sem, peers):
        pltpu.make_async_copy(box, box, sem).wait()
        flat = box.reshape(peers * PART, LANES)
        return [flat[pl.ds(j, peers, stride=PART), :] for j in range(PART)]

    def columns_of(ref, c):
        return [ref[c, :, LANES * a : LANES * (a + 1)] for a in range(8)]

    def to_columns(turn, led):
        seed = wave.at[led]
        spectrum = row_forward(
            columns_of(seed, 0), columns_of(seed, 1), turn_cos, turn_sin, halves(wide_ref)
        )
        values = [spectrum[OWNERS * j : OWNERS * (j + 1)] for j in range(2 * PART)]
        put(values[0:2] + values[4:6], col_out.at[turn, 0, led], OWNERS)
        put(values[2:4] + values[6:8], col_out.at[turn, 1, led], OWNERS)

    def column_pass(turn, half):
        tiles = arrived(col_in.at[turn, half], col_recv_sem.at[turn, half], PEERS)
        spectrum = column_forward([tiles[:2], tiles[2:]], tcol[0], tcol[1], halves(long_ref), halves(short_ref))
        real, imag = twist(spectrum[:, :LANES], spectrum[:, LANES:], filt[half, 0], filt[half, 1])
        back = column_inverse(imag, real, tcol[0], tcol[1], halves(long_ref), halves(short_ref))
        values = [
            back[PEERS * (1 - c) : PEERS * (2 - c), LANES * k : LANES * (k + 1)]
            for c in range(2)
            for k in range(2)
        ]
        put(values, row_out.at[turn, half], PEERS)
        send_rows(turn, half)

    def send_slopes(turn):
        for peer in led_peers:
            pltpu.make_async_remote_copy(
                src_ref=slope_out.at[turn, peer],
                dst_ref=slope_in.at[turn, group],
                send_sem=lsend_sem.at[turn],
                recv_sem=lrecv_sem.at[turn],
                device_id=(peer, me),
                device_id_type=MESH,
            ).start()
        pltpu.make_async_copy(
            slope_out.at[turn, group], slope_in.at[turn, group], lrecv_sem.at[turn]
        ).start()

    def from_columns(turn, led):
        layer = SLICES - 1 - turn
        first, second = [
            arrived(row_in.at[turn, half, led], row_recv_sem.at[turn, half, led], OWNERS)
            for half in range(HALVES)
        ]
        swapped = jnp.concatenate(first[2:] + second[2:] + first[:2] + second[:2], axis=0)
        imag, real = row_inverse(swapped, turn_cos, turn_sin, halves(wide_ref))
        for a in range(8):
            cols = slice(LANES * a, LANES * (a + 1))
            re, im = twist(real[a], imag[a], trans[layer, 0, :, cols], trans[layer, 1, :, cols])
            wave[led, 0, :, cols] = re
            wave[led, 1, :, cols] = im

    def slope_terms(turn, led):
        layer = SLICES - 1 - turn
        for a in range(8):
            cols = slice(LANES * a, LANES * (a + 1))
            slope_out[turn, a] += (
                fields[layer, led, 0, :, cols] * wave[led, 1, :, cols]
                - fields[layer, led, 1, :, cols] * wave[led, 0, :, cols]
            )

    slope_out[...] = jnp.zeros_like(slope_out)

    @pl.loop(0, SLICES + 1)
    def _(phase):
        @pl.loop(0, LEDS)
        def _(led):
            @pl.when(phase > 0)
            def _():
                from_columns(phase - 1, led)

            @pl.when(phase < SLICES)
            def _():
                to_columns(phase, led)

                @pl.when(phase + led == 0)
                def _():
                    pl.semaphore_wait(ready_sem, 7)

                for half in range(HALVES):
                    send_columns(phase, led, half)

            @pl.when(phase > 0)
            def _():
                slope_terms(phase - 1, led)

                @pl.when(led == LEDS - 1)
                def _():
                    send_slopes(phase - 1)

        @pl.when(phase == 0)
        def _():
            for load in loads[3:]:
                load.wait()
            for k in range(4):
                cosine, sine = filter_block(my_owner, k, led_ref[my_led])
                filt[k // 2, 0, PEERS * (k % 2) : PEERS * (k % 2 + 1), :] = cosine
                filt[k // 2, 1, PEERS * (k % 2) : PEERS * (k % 2 + 1), :] = sine
            long_ref[0], long_ref[1] = split(long_f32[...])
            short_ref[0], short_ref[1] = split(short_f32[...])
            for layer in range(SLICES):
                cosine, sine = cos_sin_turns(phases[layer] * (0.5 / math.pi))
                trans[layer, 0] = cosine
                trans[layer, 1] = sine

        @pl.when(phase < SLICES)
        def _():
            @pl.loop(0, HALVES)
            def _(half):
                column_pass(phase, half)

    for turn in range(SLICES):
        pltpu.make_async_copy(slope_in.at[turn], slope_in.at[turn], lrecv_sem.at[turn]).wait()
        slopes[SLICES - 1 - turn] = jnp.sum(slope_in[turn], axis=0) * (1.0 / (LEDS * GROUPS))
    for turn in range(SLICES):
        for half in range(HALVES):
            sent = row_out.at[turn, half, pl.ds(0, PEERS - 1)]
            for sem in (row_send_sem, col_send_sem):
                pltpu.make_async_copy(sent, sent, sem.at[turn, half]).wait()
    for turn in range(SLICES):
        sent = slope_out.at[turn, pl.ds(0, GROUPS - 1)]
        pltpu.make_async_copy(sent, sent, lsend_sem.at[turn]).wait()


def emit_kernel(slopes_in, wave_in, slopes_ref, wave_ref, sem):
    copies = [
        pltpu.make_async_copy(wave_in, wave_ref, sem.at[0]),
        pltpu.make_async_copy(slopes_in, slopes_ref, sem.at[1]),
    ]
    for copy in copies:
        copy.start()
    for copy in copies:
        copy.wait()


def local(fields, phases, residual, led_index):
    consts = [jnp.asarray(t) for t in tables()]
    scratch = [
        pltpu.SMEM(led_index.shape, jnp.int32),
        pltpu.VMEM(fields.shape, F32),
        pltpu.VMEM(phases.shape, F32),
    ]
    scratch += [pltpu.VMEM(t.shape, t.dtype) for t in consts]
    scratch += [pltpu.VMEM((2,) + t.shape, BF16) for t in consts[:3]]
    scratch += [
        pltpu.VMEM((HALVES, 2, 2 * PEERS, LANES), F32),
        pltpu.VMEM((SLICES, 2, ROWS, N), F32),
    ]
    to_col = pltpu.VMEM((SLICES, HALVES, LEDS, OWNERS, PART, LANES), F32)
    to_row = pltpu.VMEM((SLICES, HALVES, PEERS, PART, LANES), F32)
    scratch += [to_col, to_row, to_row, to_col]
    scratch += [
        pltpu.VMEM((SLICES, GROUPS, ROWS, LANES), F32),
        pltpu.VMEM((SLICES, GROUPS, ROWS, LANES), F32),
        pltpu.SemaphoreType.REGULAR,
        pltpu.SemaphoreType.DMA((9,)),
        pltpu.SemaphoreType.DMA((SLICES, HALVES)),
        pltpu.SemaphoreType.DMA((SLICES, HALVES)),
        pltpu.SemaphoreType.DMA((SLICES, HALVES)),
        pltpu.SemaphoreType.DMA((SLICES, HALVES, LEDS)),
        pltpu.SemaphoreType.DMA((SLICES,)),
        pltpu.SemaphoreType.DMA((SLICES,)),
    ]
    held = [
        pltpu.with_memory_space_constraint(x, pltpu.HBM) for x in [led_index, fields, phases, residual] + consts
    ]
    anywhere = pl.BlockSpec(memory_space=pl.ANY)
    results = pl.pallas_call(
        kernel,
        out_shape=(
            pltpu.VMEM((SLICES, ROWS, LANES), F32),
            pltpu.VMEM(residual.shape, F32),
        ),
        in_specs=[anywhere] * 9,
        out_specs=(pl.BlockSpec(memory_space=pltpu.VMEM),) * 2,
        scratch_shapes=scratch,
        compiler_params=pltpu.CompilerParams(
            collective_id=0, has_side_effects=True, vmem_limit_bytes=VMEM_LIMIT
        ),
        name="adjoint",
    )(*held)
    return pl.pallas_call(
        emit_kernel,
        out_shape=(
            pltpu.HBM((SLICES, ROWS, LANES), F32),
            pltpu.HBM(residual.shape, F32),
        ),
        in_specs=[anywhere] * 2,
        out_specs=(anywhere, anywhere),
        scratch_shapes=[pltpu.SemaphoreType.DMA((2,))],
        name="emit",
    )(*[pltpu.with_memory_space_constraint(x, pltpu.VMEM) for x in results])


def solution(mesh):
    in_specs = (
        P(None, "led", None, "row", None),
        P(None, "row", None),
        P("led", None, "row", None),
        P("led"),
    )
    out_specs = (P(None, "row", "led"), P("led", None, "row", None))
    return jax.shard_map(local, mesh=mesh, in_specs=in_specs, out_specs=out_specs, check_vma=False)
```

```python
import math

import jax
import jax.numpy as jnp
import numpy as np
from jax import lax
from jax.experimental import pallas as pl
from jax.experimental.pallas import tpu as pltpu
from jax.sharding import PartitionSpec as P

N = 1024
GRID = 15
DZ = 64
SHIFT = 10
LANES = 128
VMEM_LIMIT = 40 * 1024 * 1024
ROWS = 16
PEERS = 64
OWNERS = 32
HALVES = 2
PART = 4
GROUPS = 8
LEDS = 2
SLICES = 2
MESH = pl.DeviceIdType.MESH
F32 = jnp.float32
BF16 = jnp.bfloat16


def dft_block(length):
    index = np.arange(length)
    angle = 2.0 * np.pi * (np.outer(index, index) % length) / length
    return np.cos(angle), np.sin(angle)


def complex_left(length):
    cos, sin = dft_block(length)
    return np.block([[cos, sin], [-sin, cos]])


def tables():
    wide = complex_left(LANES).astype(np.float32)
    long = complex_left(PEERS).astype(np.float32)
    cos, sin = dft_block(ROWS)
    eye = np.eye(LANES // ROWS)
    cos, sin = np.kron(eye, cos), np.kron(eye, sin)
    short = np.block([[cos, -sin], [sin, cos]]).astype(np.float32)
    angle = 2.0 * np.pi * np.outer(np.arange(8), np.arange(LANES)) / N
    turn_rows = np.concatenate([np.cos(angle), np.sin(angle)]).astype(np.float32)
    angle = 2.0 * np.pi * np.outer(np.arange(PEERS), np.arange(LANES) % ROWS) / N
    turn_cols = np.stack([np.cos(angle), np.sin(angle)]).astype(np.float32)
    return wide, long, short, turn_rows, turn_cols


def fit_turns():
    nodes = 0.5 * np.cos(np.pi * (np.arange(400) + 0.5) / 800)
    square = nodes * nodes
    basis = np.vander(square, 8, increasing=True)
    sin_fit = np.linalg.lstsq(basis, np.sin(2 * np.pi * nodes) / nodes, rcond=None)[0]
    cos_fit = np.linalg.lstsq(basis, np.cos(2 * np.pi * nodes), rcond=None)[0]
    return [float(v) for v in sin_fit], [float(v) for v in cos_fit]


SIN_FIT, COS_FIT = fit_turns()


def cos_sin_turns(turns):
    frac = turns - jnp.floor(turns + 0.5)
    square = frac * frac
    sine = jnp.full_like(square, SIN_FIT[-1])
    cosine = jnp.full_like(square, COS_FIT[-1])
    for s, c in zip(SIN_FIT[-2::-1], COS_FIT[-2::-1]):
        sine = sine * square + s
        cosine = cosine * square + c
    return cosine, sine * frac


def split(value):
    high = value.astype(BF16)
    return high, (value - high.astype(F32)).astype(BF16)


def dot3(left, right, dims):
    def dot(a, b):
        return lax.dot_general(a, b, (dims, ((), ())), preferred_element_type=F32)

    return dot(left[0], right[0]) + (dot(left[0], right[1]) + dot(left[1], right[0]))


def radix8(real, imag):
    half = math.sqrt(0.5)

    def pair(a, b):
        return (a[0] + b[0], a[1] + b[1]), (a[0] - b[0], a[1] - b[1])

    def minus_i(a):
        return a[1], -a[0]

    def four(z):
        s0, d0 = pair(z[0], z[2])
        s1, d1 = pair(z[1], z[3])
        y0, y2 = pair(s0, s1)
        y1, y3 = pair(d0, minus_i(d1))
        return [y0, y1, y2, y3]

    z = list(zip(real, imag))
    even = four([z[0], z[2], z[4], z[6]])
    odd = four([z[1], z[3], z[5], z[7]])
    odd[1] = ((odd[1][0] + odd[1][1]) * half, (odd[1][1] - odd[1][0]) * half)
    odd[2] = minus_i(odd[2])
    odd[3] = ((odd[3][1] - odd[3][0]) * half, (odd[3][0] + odd[3][1]) * -half)
    out = [None] * 8
    for k in range(4):
        out[k], out[k + 4] = pair(even[k], odd[k])
    return [o[0] for o in out], [o[1] for o in out]


def twist(real, imag, cos, sin):
    return real * cos + imag * sin, imag * cos - real * sin


def row_forward(real, imag, turn_cos, turn_sin, wide):
    real, imag = radix8(real, imag)
    rows = []
    for k in range(8):
        re, im = (real[k], imag[k]) if k == 0 else twist(real[k], imag[k], turn_cos[k], turn_sin[k])
        rows.append(jnp.concatenate([re, im], axis=1))
    return dot3(wide, split(jnp.concatenate(rows, axis=0)), ((1,), (1,)))


def row_inverse(swapped, turn_cos, turn_sin, wide):
    spread = dot3(wide, split(swapped), ((1,), (0,)))
    first = spread[:LANES].T
    second = spread[LANES:].T
    real, imag = [], []
    for k in range(8):
        re, im = first[ROWS * k : ROWS * (k + 1)], second[ROWS * k : ROWS * (k + 1)]
        if k > 0:
            re, im = twist(re, im, turn_cos[k], turn_sin[k])
        real.append(re)
        imag.append(im)
    return radix8(real, imag)


def column_forward(blocks, turn_cos, turn_sin, long, short):
    stacked = jnp.concatenate([jnp.concatenate(blocks[c], axis=1) for c in range(2)], axis=0)
    mixed = dot3(long, split(stacked), ((1,), (0,)))
    rows = []
    for k in range(2):
        re = mixed[:PEERS, LANES * k : LANES * (k + 1)]
        im = mixed[PEERS:, LANES * k : LANES * (k + 1)]
        rows.append(jnp.concatenate(twist(re, im, turn_cos, turn_sin), axis=1))
    return dot3(split(jnp.concatenate(rows, axis=0)), short, ((1,), (0,)))


def column_inverse(real, imag, turn_cos, turn_sin, long, short):
    mixed = dot3(split(jnp.concatenate([real, imag], axis=1)), short, ((1,), (0,)))
    first, second = [], []
    for k in range(2):
        block = mixed[PEERS * k : PEERS * (k + 1)]
        re, im = twist(block[:, :LANES], block[:, LANES:], turn_cos, turn_sin)
        first.append(re)
        second.append(im)
    stacked = jnp.concatenate(
        [jnp.concatenate(first, axis=1), jnp.concatenate(second, axis=1)], axis=0
    )
    return dot3(long, split(stacked), ((1,), (0,)))


def filter_block(owner, k2lo, led):
    lane = lax.broadcasted_iota(jnp.int32, (PEERS, LANES), 1)
    v1 = lax.broadcasted_iota(jnp.int32, (PEERS, LANES), 0)
    u = (lane >> 4) + 8 * (OWNERS * k2lo + owner)
    v = v1 + PEERS * (lane & (ROWS - 1))
    kx = (led // GRID - GRID // 2) * SHIFT
    ky = (led % GRID - GRID // 2) * SHIFT
    fx = (((u + N // 2) & (N - 1)) - N // 2 + kx).astype(F32) * (1.0 / N)
    fy = (((v + N // 2) & (N - 1)) - N // 2 + ky).astype(F32) * (1.0 / N)
    turns = DZ * (jnp.sqrt(1.0 - fx * fx - fy * fy) - 1.0)
    cosine, sine = cos_sin_turns(turns)
    return cosine * (1.0 / (N * N)), sine * (1.0 / (N * N))


def kernel(
    led_hbm, fields_hbm, phases_hbm, residual_hbm, wide_hbm, long_hbm, short_hbm, trow_hbm, tcol_hbm,
    slopes, wave,
    led_ref, fields, phases, wide_f32, long_f32, short_f32, trow, tcol, wide_ref, long_ref, short_ref,
    filt, trans, col_out, col_in, row_out, row_in, slope_out, slope_in,
    load_sem, col_send_sem, col_recv_sem, row_send_sem, row_recv_sem, lsend_sem, lrecv_sem,
):
    me = lax.axis_index("row")
    group = lax.axis_index("led")
    my_y, my_w = me // 8, me % 8
    my_x, my_z = my_w // 2, my_w % 2
    my_led = lax.rem(my_x + my_y, 2)
    my_owner = my_y * 4 + my_x // 2 * 2 + my_z
    led_peers = [lax.rem(group + d, GROUPS) for d in (4, 3, 5, 2, 6, 7, 1)]

    loads = [
        pltpu.make_async_copy(src, dst, load_sem.at[n])
        for n, (src, dst) in enumerate(
            [
                (residual_hbm, wave),
                (trow_hbm, trow),
                (wide_hbm, wide_f32),
                (tcol_hbm, tcol),
                (long_hbm, long_f32),
                (short_hbm, short_f32),
                (phases_hbm, phases),
                (fields_hbm, fields),
                (led_hbm, led_ref),
            ]
        )
    ]
    for load in loads:
        load.start()

    barrier = pltpu.get_barrier_semaphore()

    @pl.loop(1, PEERS)
    def _(step):
        peer = lax.rem(me + step, PEERS)
        pl.semaphore_signal(barrier, inc=1, device_id=(group, peer), device_id_type=MESH)

    for peer in led_peers:
        pl.semaphore_signal(barrier, inc=1, device_id=(peer, me), device_id_type=MESH)

    for load in loads[:3]:
        load.wait()
    turn_cos = [trow[k : k + 1, :] for k in range(8)]
    turn_sin = [trow[8 + k : 9 + k, :] for k in range(8)]
    wide_ref[0], wide_ref[1] = split(wide_f32[...])

    def halves(table):
        return table[0], table[1]

    way = 1 - 2 * lax.rem(group, 2)
    ys = [lax.rem(my_y + 8 + way * dy, 8) for dy in range(8)]
    xs = [lax.rem(my_x + 4 + way * dx, 4) for dx in range(4)]

    def away(step, ring):
        return min(step, ring - step)

    owner_steps = sorted(
        [(dy, dx, dz) for dy in (4, 3, 5, 2, 6, 1, 7, 0) for dx in (1, 0) for dz in (1, 0)],
        key=lambda step: -(away(step[0], 8) + 1.5 * step[1] + step[2]),
    )[:-1]
    row_steps = sorted(
        [(dy, dx, dz) for dy in (4, 3, 5, 2, 6, 1, 7, 0) for dx in (2, 1, 3, 0) for dz in (1, 0)],
        key=lambda step: -(away(step[0], 8) + away(step[1], 4) + step[2]),
    )[:-1]

    def copy_tile(source, target, send_sem, recv_sem, peer):
        pltpu.make_async_remote_copy(
            src_ref=source,
            dst_ref=target,
            send_sem=send_sem,
            recv_sem=recv_sem,
            device_id=(group, peer),
            device_id_type=MESH,
        ).start()

    def send_columns(turn, led, half):
        target = col_in.at[turn, half, me]
        sem = col_recv_sem.at[turn, half]
        sent = col_send_sem.at[turn, half]

        def to(dy, dx, dz):
            y, pair, z = ys[dy], lax.rem(my_x // 2 + dx, 2), lax.rem(my_z + dz, 2)
            source = col_out.at[turn, half, led, y * 4 + pair * 2 + z]
            return source, y * 8 + pair * 4 + lax.rem(led + y, 2) * 2 + z

        for step in owner_steps:
            source, peer = to(*step)
            copy_tile(source, target, sent, sem, peer)
        source, peer = to(0, 0, 0)

        @pl.when(led == my_led)
        def _():
            pltpu.make_async_copy(source, target, sem).start()

        @pl.when(led != my_led)
        def _():
            copy_tile(source, target, sent, sem, peer)

    def send_rows(turn, half):
        target = row_in.at[turn, half, my_led, my_owner]
        sem = row_recv_sem.at[turn, half, my_led]
        for dy, dx, dz in row_steps:
            y, x, z = ys[dy], xs[dx], lax.rem(my_z + dz, 2)
            peer = y * 8 + x * 2 + z
            copy_tile(row_out.at[turn, half, peer], target, row_send_sem.at[turn, half], sem, peer)
        pltpu.make_async_copy(row_out.at[turn, half, me], target, sem).start()

    def put(values, box, peers):
        flat = box.reshape(peers * PART, LANES)
        for j in range(PART):
            flat[pl.ds(j, peers, stride=PART), :] = values[j]

    def arrived(box, sem, peers):
        pltpu.make_async_copy(box, box, sem).wait()
        flat = box.reshape(peers * PART, LANES)
        return [flat[pl.ds(j, peers, stride=PART), :] for j in range(PART)]

    def columns_of(ref, c):
        return [ref[c, :, LANES * a : LANES * (a + 1)] for a in range(8)]

    def to_columns(turn, led):
        seed = wave.at[led]
        spectrum = row_forward(
            columns_of(seed, 0), columns_of(seed, 1), turn_cos, turn_sin, halves(wide_ref)
        )
        values = [spectrum[OWNERS * j : OWNERS * (j + 1)] for j in range(2 * PART)]
        put(values[0:2] + values[4:6], col_out.at[turn, 0, led], OWNERS)
        put(values[2:4] + values[6:8], col_out.at[turn, 1, led], OWNERS)

    def column_pass(turn, half):
        tiles = arrived(col_in.at[turn, half], col_recv_sem.at[turn, half], PEERS)
        spectrum = column_forward([tiles[:2], tiles[2:]], tcol[0], tcol[1], halves(long_ref), halves(short_ref))
        real, imag = twist(spectrum[:, :LANES], spectrum[:, LANES:], filt[half, 0], filt[half, 1])
        back = column_inverse(imag, real, tcol[0], tcol[1], halves(long_ref), halves(short_ref))
        values = [
            back[PEERS * (1 - c) : PEERS * (2 - c), LANES * k : LANES * (k + 1)]
            for c in range(2)
            for k in range(2)
        ]
        put(values, row_out.at[turn, half], PEERS)
        send_rows(turn, half)

    def send_slopes(turn):
        for peer in led_peers:
            pltpu.make_async_remote_copy(
                src_ref=slope_out.at[turn, peer],
                dst_ref=slope_in.at[turn, group],
                send_sem=lsend_sem.at[turn],
                recv_sem=lrecv_sem.at[turn],
                device_id=(peer, me),
                device_id_type=MESH,
            ).start()
        pltpu.make_async_copy(
            slope_out.at[turn, group], slope_in.at[turn, group], lrecv_sem.at[turn]
        ).start()

    def from_columns(turn, led):
        layer = SLICES - 1 - turn
        first, second = [
            arrived(row_in.at[turn, half, led], row_recv_sem.at[turn, half, led], OWNERS)
            for half in range(HALVES)
        ]
        swapped = jnp.concatenate(first[2:] + second[2:] + first[:2] + second[:2], axis=0)
        imag, real = row_inverse(swapped, turn_cos, turn_sin, halves(wide_ref))
        for a in range(8):
            cols = slice(LANES * a, LANES * (a + 1))
            re, im = twist(real[a], imag[a], trans[layer, 0, :, cols], trans[layer, 1, :, cols])
            wave[led, 0, :, cols] = re
            wave[led, 1, :, cols] = im

    def slope_terms(turn, led):
        layer = SLICES - 1 - turn
        for a in range(8):
            cols = slice(LANES * a, LANES * (a + 1))
            slope_out[turn, a] += (
                fields[layer, led, 0, :, cols] * wave[led, 1, :, cols]
                - fields[layer, led, 1, :, cols] * wave[led, 0, :, cols]
            )

    slope_out[...] = jnp.zeros_like(slope_out)

    @pl.loop(0, SLICES + 1)
    def _(phase):
        @pl.loop(0, LEDS)
        def _(led):
            @pl.when(phase > 0)
            def _():
                from_columns(phase - 1, led)

            @pl.when(phase < SLICES)
            def _():
                to_columns(phase, led)

                @pl.when(phase + led == 0)
                def _():
                    pl.semaphore_wait(barrier, PEERS - 1 + GROUPS - 1)

                for half in range(HALVES):
                    send_columns(phase, led, half)

            @pl.when(phase > 0)
            def _():
                slope_terms(phase - 1, led)

                @pl.when(led == LEDS - 1)
                def _():
                    send_slopes(phase - 1)

        @pl.when(phase == 0)
        def _():
            for load in loads[3:]:
                load.wait()
            for k in range(4):
                cosine, sine = filter_block(my_owner, k, led_ref[my_led])
                filt[k // 2, 0, PEERS * (k % 2) : PEERS * (k % 2 + 1), :] = cosine
                filt[k // 2, 1, PEERS * (k % 2) : PEERS * (k % 2 + 1), :] = sine
            long_ref[0], long_ref[1] = split(long_f32[...])
            short_ref[0], short_ref[1] = split(short_f32[...])
            for layer in range(SLICES):
                cosine, sine = cos_sin_turns(phases[layer] * (0.5 / math.pi))
                trans[layer, 0] = cosine
                trans[layer, 1] = sine

        @pl.when(phase < SLICES)
        def _():
            @pl.loop(0, HALVES)
            def _(half):
                column_pass(phase, half)

    for turn in range(SLICES):
        pltpu.make_async_copy(slope_in.at[turn], slope_in.at[turn], lrecv_sem.at[turn]).wait()
        slopes[SLICES - 1 - turn] = jnp.sum(slope_in[turn], axis=0) * (1.0 / (LEDS * GROUPS))
    for turn in range(SLICES):
        for half in range(HALVES):
            sent = row_out.at[turn, half, pl.ds(0, PEERS - 1)]
            for sem in (row_send_sem, col_send_sem):
                pltpu.make_async_copy(sent, sent, sem.at[turn, half]).wait()
    for turn in range(SLICES):
        sent = slope_out.at[turn, pl.ds(0, GROUPS - 1)]
        pltpu.make_async_copy(sent, sent, lsend_sem.at[turn]).wait()


def emit_kernel(slopes_in, wave_in, slopes_ref, wave_ref, sem):
    copies = [
        pltpu.make_async_copy(wave_in, wave_ref, sem.at[0]),
        pltpu.make_async_copy(slopes_in, slopes_ref, sem.at[1]),
    ]
    for copy in copies:
        copy.start()
    for copy in copies:
        copy.wait()


def local(fields, phases, residual, led_index):
    consts = [jnp.asarray(t) for t in tables()]
    scratch = [
        pltpu.SMEM(led_index.shape, jnp.int32),
        pltpu.VMEM(fields.shape, F32),
        pltpu.VMEM(phases.shape, F32),
    ]
    scratch += [pltpu.VMEM(t.shape, t.dtype) for t in consts]
    scratch += [pltpu.VMEM((2,) + t.shape, BF16) for t in consts[:3]]
    scratch += [
        pltpu.VMEM((HALVES, 2, 2 * PEERS, LANES), F32),
        pltpu.VMEM((SLICES, 2, ROWS, N), F32),
    ]
    to_col = pltpu.VMEM((SLICES, HALVES, LEDS, OWNERS, PART, LANES), F32)
    to_row = pltpu.VMEM((SLICES, HALVES, PEERS, PART, LANES), F32)
    scratch += [to_col, to_row, to_row, to_col]
    scratch += [
        pltpu.VMEM((SLICES, GROUPS, ROWS, LANES), F32),
        pltpu.VMEM((SLICES, GROUPS, ROWS, LANES), F32),
        pltpu.SemaphoreType.DMA((9,)),
        pltpu.SemaphoreType.DMA((SLICES, HALVES)),
        pltpu.SemaphoreType.DMA((SLICES, HALVES)),
        pltpu.SemaphoreType.DMA((SLICES, HALVES)),
        pltpu.SemaphoreType.DMA((SLICES, HALVES, LEDS)),
        pltpu.SemaphoreType.DMA((SLICES,)),
        pltpu.SemaphoreType.DMA((SLICES,)),
    ]
    held = [
        pltpu.with_memory_space_constraint(x, pltpu.HBM) for x in [led_index, fields, phases, residual] + consts
    ]
    anywhere = pl.BlockSpec(memory_space=pl.ANY)
    results = pl.pallas_call(
        kernel,
        out_shape=(
            pltpu.VMEM((SLICES, ROWS, LANES), F32),
            pltpu.VMEM(residual.shape, F32),
        ),
        in_specs=[anywhere] * 9,
        out_specs=(pl.BlockSpec(memory_space=pltpu.VMEM),) * 2,
        scratch_shapes=scratch,
        compiler_params=pltpu.CompilerParams(
            collective_id=0, has_side_effects=True, vmem_limit_bytes=VMEM_LIMIT
        ),
        name="adjoint",
    )(*held)
    return pl.pallas_call(
        emit_kernel,
        out_shape=(
            pltpu.HBM((SLICES, ROWS, LANES), F32),
            pltpu.HBM(residual.shape, F32),
        ),
        in_specs=[anywhere] * 2,
        out_specs=(anywhere, anywhere),
        scratch_shapes=[pltpu.SemaphoreType.DMA((2,))],
        name="emit",
    )(*[pltpu.with_memory_space_constraint(x, pltpu.VMEM) for x in results])


def solution(mesh):
    in_specs = (
        P(None, "led", None, "row", None),
        P(None, "row", None),
        P("led", None, "row", None),
        P("led"),
    )
    out_specs = (P(None, "row", "led"), P("led", None, "row", None))
    return jax.shard_map(local, mesh=mesh, in_specs=in_specs, out_specs=out_specs, check_vma=False)
```

```python
import math

import jax
import jax.numpy as jnp
import numpy as np
from jax import lax
from jax.experimental import pallas as pl
from jax.experimental.pallas import tpu as pltpu
from jax.sharding import PartitionSpec as P

N = 1024
GRID = 15
DZ = 64
SHIFT = 10
LANES = 128
VMEM_LIMIT = 40 * 1024 * 1024
ROWS = 16
PEERS = 64
OWNERS = 32
HALVES = 2
PART = 4
GROUPS = 8
LEDS = 2
SLICES = 2
MESH = pl.DeviceIdType.MESH
F32 = jnp.float32
BF16 = jnp.bfloat16


def dft_block(length):
    index = np.arange(length)
    angle = 2.0 * np.pi * (np.outer(index, index) % length) / length
    return np.cos(angle), np.sin(angle)


def complex_left(length):
    cos, sin = dft_block(length)
    return np.block([[cos, sin], [-sin, cos]])


def tables():
    wide = complex_left(LANES).astype(np.float32)
    long = complex_left(PEERS).astype(np.float32)
    cos, sin = dft_block(ROWS)
    eye = np.eye(LANES // ROWS)
    cos, sin = np.kron(eye, cos), np.kron(eye, sin)
    short = np.block([[cos, -sin], [sin, cos]]).astype(np.float32)
    angle = 2.0 * np.pi * np.outer(np.arange(8), np.arange(LANES)) / N
    turn_rows = np.concatenate([np.cos(angle), np.sin(angle)]).astype(np.float32)
    angle = 2.0 * np.pi * np.outer(np.arange(PEERS), np.arange(LANES) % ROWS) / N
    turn_cols = np.stack([np.cos(angle), np.sin(angle)]).astype(np.float32)
    return wide, long, short, turn_rows, turn_cols


def fit_turns():
    nodes = 0.5 * np.cos(np.pi * (np.arange(400) + 0.5) / 800)
    square = nodes * nodes
    basis = np.vander(square, 8, increasing=True)
    sin_fit = np.linalg.lstsq(basis, np.sin(2 * np.pi * nodes) / nodes, rcond=None)[0]
    cos_fit = np.linalg.lstsq(basis, np.cos(2 * np.pi * nodes), rcond=None)[0]
    return [float(v) for v in sin_fit], [float(v) for v in cos_fit]


SIN_FIT, COS_FIT = fit_turns()


def cos_sin_turns(turns):
    frac = turns - jnp.floor(turns + 0.5)
    square = frac * frac
    sine = jnp.full_like(square, SIN_FIT[-1])
    cosine = jnp.full_like(square, COS_FIT[-1])
    for s, c in zip(SIN_FIT[-2::-1], COS_FIT[-2::-1]):
        sine = sine * square + s
        cosine = cosine * square + c
    return cosine, sine * frac


def split(value):
    high = value.astype(BF16)
    return high, (value - high.astype(F32)).astype(BF16)


def dot3(left, right, dims):
    def dot(a, b):
        return lax.dot_general(a, b, (dims, ((), ())), preferred_element_type=F32)

    return dot(left[0], right[0]) + (dot(left[0], right[1]) + dot(left[1], right[0]))


def radix8(real, imag):
    half = math.sqrt(0.5)

    def pair(a, b):
        return (a[0] + b[0], a[1] + b[1]), (a[0] - b[0], a[1] - b[1])

    def minus_i(a):
        return a[1], -a[0]

    def four(z):
        s0, d0 = pair(z[0], z[2])
        s1, d1 = pair(z[1], z[3])
        y0, y2 = pair(s0, s1)
        y1, y3 = pair(d0, minus_i(d1))
        return [y0, y1, y2, y3]

    z = list(zip(real, imag))
    even = four([z[0], z[2], z[4], z[6]])
    odd = four([z[1], z[3], z[5], z[7]])
    odd[1] = ((odd[1][0] + odd[1][1]) * half, (odd[1][1] - odd[1][0]) * half)
    odd[2] = minus_i(odd[2])
    odd[3] = ((odd[3][1] - odd[3][0]) * half, (odd[3][0] + odd[3][1]) * -half)
    out = [None] * 8
    for k in range(4):
        out[k], out[k + 4] = pair(even[k], odd[k])
    return [o[0] for o in out], [o[1] for o in out]


def twist(real, imag, cos, sin):
    return real * cos + imag * sin, imag * cos - real * sin


def row_forward(real, imag, turn_cos, turn_sin, wide):
    real, imag = radix8(real, imag)
    rows = []
    for k in range(8):
        re, im = (real[k], imag[k]) if k == 0 else twist(real[k], imag[k], turn_cos[k], turn_sin[k])
        rows.append(jnp.concatenate([re, im], axis=1))
    waves = split(jnp.concatenate(rows, axis=0))
    for low in (0, LANES // 2):
        part = [
            jnp.concatenate([w[low : low + LANES // 2], w[LANES + low : LANES + low + LANES // 2]], axis=0)
            for w in wide
        ]
        yield dot3(part, waves, ((1,), (1,)))


def row_inverse(swapped, turn_cos, turn_sin, wide):
    spread = dot3(wide, split(swapped), ((1,), (0,)))
    first = spread[:LANES].T
    second = spread[LANES:].T
    real, imag = [], []
    for k in range(8):
        re, im = first[ROWS * k : ROWS * (k + 1)], second[ROWS * k : ROWS * (k + 1)]
        if k > 0:
            re, im = twist(re, im, turn_cos[k], turn_sin[k])
        real.append(re)
        imag.append(im)
    return radix8(real, imag)


def column_forward(blocks, turn_cos, turn_sin, long, short):
    stacked = jnp.concatenate([jnp.concatenate(blocks[c], axis=1) for c in range(2)], axis=0)
    mixed = dot3(long, split(stacked), ((1,), (0,)))
    rows = []
    for k in range(2):
        re = mixed[:PEERS, LANES * k : LANES * (k + 1)]
        im = mixed[PEERS:, LANES * k : LANES * (k + 1)]
        rows.append(jnp.concatenate(twist(re, im, turn_cos, turn_sin), axis=1))
    return dot3(split(jnp.concatenate(rows, axis=0)), short, ((1,), (0,)))


def column_inverse(real, imag, turn_cos, turn_sin, long, short):
    mixed = dot3(split(jnp.concatenate([real, imag], axis=1)), short, ((1,), (0,)))
    first, second = [], []
    for k in range(2):
        block = mixed[PEERS * k : PEERS * (k + 1)]
        re, im = twist(block[:, :LANES], block[:, LANES:], turn_cos, turn_sin)
        first.append(re)
        second.append(im)
    stacked = jnp.concatenate(
        [jnp.concatenate(first, axis=1), jnp.concatenate(second, axis=1)], axis=0
    )
    return dot3(long, split(stacked), ((1,), (0,)))


def filter_block(owner, k2lo, led):
    lane = lax.broadcasted_iota(jnp.int32, (PEERS, LANES), 1)
    v1 = lax.broadcasted_iota(jnp.int32, (PEERS, LANES), 0)
    u = (lane >> 4) + 8 * (OWNERS * k2lo + owner)
    v = v1 + PEERS * (lane & (ROWS - 1))
    kx = (led // GRID - GRID // 2) * SHIFT
    ky = (led % GRID - GRID // 2) * SHIFT
    fx = (((u + N // 2) & (N - 1)) - N // 2 + kx).astype(F32) * (1.0 / N)
    fy = (((v + N // 2) & (N - 1)) - N // 2 + ky).astype(F32) * (1.0 / N)
    turns = DZ * (jnp.sqrt(1.0 - fx * fx - fy * fy) - 1.0)
    cosine, sine = cos_sin_turns(turns)
    return cosine * (1.0 / (N * N)), sine * (1.0 / (N * N))


def kernel(
    led_hbm, fields_hbm, phases_hbm, residual_hbm, wide_hbm, long_hbm, short_hbm, trow_hbm, tcol_hbm,
    slopes, wave,
    led_ref, fields, phases, wide_f32, long_f32, short_f32, trow, tcol, wide_ref, long_ref, short_ref,
    filt, trans, col_out, col_in, row_out, row_in, slope_out, slope_in,
    load_sem, col_send_sem, col_recv_sem, row_send_sem, row_recv_sem, lsend_sem, lrecv_sem,
):
    me = lax.axis_index("row")
    group = lax.axis_index("led")
    my_y, my_w = me // 8, me % 8
    my_x, my_z = my_w // 2, my_w % 2
    my_led = lax.rem(my_x + my_y, 2)
    my_owner = my_y * 4 + my_x // 2 * 2 + my_z
    led_peers = [lax.rem(group + d, GROUPS) for d in (4, 3, 5, 2, 6, 7, 1)]

    loads = [
        pltpu.make_async_copy(src, dst, load_sem.at[n])
        for n, (src, dst) in enumerate(
            [
                (residual_hbm, wave),
                (trow_hbm, trow),
                (wide_hbm, wide_f32),
                (tcol_hbm, tcol),
                (long_hbm, long_f32),
                (short_hbm, short_f32),
                (phases_hbm, phases),
                (fields_hbm, fields),
                (led_hbm, led_ref),
            ]
        )
    ]
    for load in loads:
        load.start()

    barrier = pltpu.get_barrier_semaphore()

    @pl.loop(1, PEERS)
    def _(step):
        peer = lax.rem(me + step, PEERS)
        pl.semaphore_signal(barrier, inc=1, device_id=(group, peer), device_id_type=MESH)

    for peer in led_peers:
        pl.semaphore_signal(barrier, inc=1, device_id=(peer, me), device_id_type=MESH)

    for load in loads[:3]:
        load.wait()
    turn_cos = [trow[k : k + 1, :] for k in range(8)]
    turn_sin = [trow[8 + k : 9 + k, :] for k in range(8)]
    wide_ref[0], wide_ref[1] = split(wide_f32[...])

    def halves(table):
        return table[0], table[1]

    way = 1 - 2 * lax.rem(group, 2)
    ys = [lax.rem(my_y + 8 + way * dy, 8) for dy in range(8)]
    xs = [lax.rem(my_x + 4 + way * dx, 4) for dx in range(4)]

    def away(step, ring):
        return min(step, ring - step)

    owner_steps = sorted(
        [(dy, dx, dz) for dy in (4, 3, 5, 2, 6, 1, 7, 0) for dx in (1, 0) for dz in (1, 0)],
        key=lambda step: -(away(step[0], 8) + 1.5 * step[1] + step[2]),
    )[:-1]
    row_steps = sorted(
        [(dy, dx, dz) for dy in (4, 3, 5, 2, 6, 1, 7, 0) for dx in (2, 1, 3, 0) for dz in (1, 0)],
        key=lambda step: -(away(step[0], 8) + away(step[1], 4) + step[2]),
    )[:-1]

    def copy_tile(source, target, send_sem, recv_sem, peer):
        pltpu.make_async_remote_copy(
            src_ref=source,
            dst_ref=target,
            send_sem=send_sem,
            recv_sem=recv_sem,
            device_id=(group, peer),
            device_id_type=MESH,
        ).start()

    def send_columns(turn, led, half):
        target = col_in.at[turn, half, me]
        sem = col_recv_sem.at[turn, half]
        sent = col_send_sem.at[turn, half]

        def to(dy, dx, dz):
            y, pair, z = ys[dy], lax.rem(my_x // 2 + dx, 2), lax.rem(my_z + dz, 2)
            source = col_out.at[turn, half, led, y * 4 + pair * 2 + z]
            return source, y * 8 + pair * 4 + lax.rem(led + y, 2) * 2 + z

        for step in owner_steps:
            source, peer = to(*step)
            copy_tile(source, target, sent, sem, peer)
        source, peer = to(0, 0, 0)

        @pl.when(led == my_led)
        def _():
            pltpu.make_async_copy(source, target, sem).start()

        @pl.when(led != my_led)
        def _():
            copy_tile(source, target, sent, sem, peer)

    def send_rows(turn, half):
        target = row_in.at[turn, half, my_led, my_owner]
        sem = row_recv_sem.at[turn, half, my_led]
        for dy, dx, dz in row_steps:
            y, x, z = ys[dy], xs[dx], lax.rem(my_z + dz, 2)
            peer = y * 8 + x * 2 + z
            copy_tile(row_out.at[turn, half, peer], target, row_send_sem.at[turn, half], sem, peer)
        pltpu.make_async_copy(row_out.at[turn, half, me], target, sem).start()

    def put(values, box, peers):
        flat = box.reshape(peers * PART, LANES)
        for j in range(PART):
            flat[pl.ds(j, peers, stride=PART), :] = values[j]

    def arrived(box, sem, peers):
        pltpu.make_async_copy(box, box, sem).wait()
        flat = box.reshape(peers * PART, LANES)
        return [flat[pl.ds(j, peers, stride=PART), :] for j in range(PART)]

    def columns_of(ref, c):
        return [ref[c, :, LANES * a : LANES * (a + 1)] for a in range(8)]

    def to_columns(turn, led):
        seed = wave.at[led]
        spectra = row_forward(
            columns_of(seed, 0), columns_of(seed, 1), turn_cos, turn_sin, halves(wide_ref)
        )
        for half, spectrum in enumerate(spectra):
            values = [spectrum[OWNERS * j : OWNERS * (j + 1)] for j in range(PART)]
            put(values, col_out.at[turn, half, led], OWNERS)
            if half == 0:
                @pl.when(turn + led == 0)
                def _():
                    pl.semaphore_wait(barrier, PEERS - 1 + GROUPS - 1)

            send_columns(turn, led, half)

    def column_pass(turn, half):
        tiles = arrived(col_in.at[turn, half], col_recv_sem.at[turn, half], PEERS)
        spectrum = column_forward([tiles[:2], tiles[2:]], tcol[0], tcol[1], halves(long_ref), halves(short_ref))
        real, imag = twist(spectrum[:, :LANES], spectrum[:, LANES:], filt[half, 0], filt[half, 1])
        back = column_inverse(imag, real, tcol[0], tcol[1], halves(long_ref), halves(short_ref))
        values = [
            back[PEERS * (1 - c) : PEERS * (2 - c), LANES * k : LANES * (k + 1)]
            for c in range(2)
            for k in range(2)
        ]
        put(values, row_out.at[turn, half], PEERS)
        send_rows(turn, half)

    def send_slopes(turn):
        for peer in led_peers:
            pltpu.make_async_remote_copy(
                src_ref=slope_out.at[turn, peer],
                dst_ref=slope_in.at[turn, group],
                send_sem=lsend_sem.at[turn],
                recv_sem=lrecv_sem.at[turn],
                device_id=(peer, me),
                device_id_type=MESH,
            ).start()
        pltpu.make_async_copy(
            slope_out.at[turn, group], slope_in.at[turn, group], lrecv_sem.at[turn]
        ).start()

    def from_columns(turn, led):
        layer = SLICES - 1 - turn
        first, second = [
            arrived(row_in.at[turn, half, led], row_recv_sem.at[turn, half, led], OWNERS)
            for half in range(HALVES)
        ]
        swapped = jnp.concatenate(first[2:] + second[2:] + first[:2] + second[:2], axis=0)
        imag, real = row_inverse(swapped, turn_cos, turn_sin, halves(wide_ref))
        for a in range(8):
            cols = slice(LANES * a, LANES * (a + 1))
            re, im = twist(real[a], imag[a], trans[layer, 0, :, cols], trans[layer, 1, :, cols])
            wave[led, 0, :, cols] = re
            wave[led, 1, :, cols] = im

    def slope_terms(turn, led):
        layer = SLICES - 1 - turn
        for a in range(8):
            cols = slice(LANES * a, LANES * (a + 1))
            slope_out[turn, a] += (
                fields[layer, led, 0, :, cols] * wave[led, 1, :, cols]
                - fields[layer, led, 1, :, cols] * wave[led, 0, :, cols]
            )

    slope_out[...] = jnp.zeros_like(slope_out)

    @pl.loop(0, SLICES + 1)
    def _(phase):
        @pl.loop(0, LEDS)
        def _(led):
            @pl.when(phase > 0)
            def _():
                from_columns(phase - 1, led)

            @pl.when(phase < SLICES)
            def _():
                to_columns(phase, led)

            @pl.when(phase > 0)
            def _():
                slope_terms(phase - 1, led)

                @pl.when(led == LEDS - 1)
                def _():
                    send_slopes(phase - 1)

        @pl.when(phase == 0)
        def _():
            for load in loads[3:]:
                load.wait()
            for k in range(4):
                cosine, sine = filter_block(my_owner, k, led_ref[my_led])
                filt[k // 2, 0, PEERS * (k % 2) : PEERS * (k % 2 + 1), :] = cosine
                filt[k // 2, 1, PEERS * (k % 2) : PEERS * (k % 2 + 1), :] = sine
            long_ref[0], long_ref[1] = split(long_f32[...])
            short_ref[0], short_ref[1] = split(short_f32[...])
            for layer in range(SLICES):
                cosine, sine = cos_sin_turns(phases[layer] * (0.5 / math.pi))
                trans[layer, 0] = cosine
                trans[layer, 1] = sine

        @pl.when(phase < SLICES)
        def _():
            @pl.loop(0, HALVES)
            def _(half):
                column_pass(phase, half)

    for turn in range(SLICES):
        pltpu.make_async_copy(slope_in.at[turn], slope_in.at[turn], lrecv_sem.at[turn]).wait()
        slopes[SLICES - 1 - turn] = jnp.sum(slope_in[turn], axis=0) * (1.0 / (LEDS * GROUPS))
    for turn in range(SLICES):
        for half in range(HALVES):
            sent = row_out.at[turn, half, pl.ds(0, PEERS - 1)]
            for sem in (row_send_sem, col_send_sem):
                pltpu.make_async_copy(sent, sent, sem.at[turn, half]).wait()
    for turn in range(SLICES):
        sent = slope_out.at[turn, pl.ds(0, GROUPS - 1)]
        pltpu.make_async_copy(sent, sent, lsend_sem.at[turn]).wait()


def emit_kernel(slopes_in, wave_in, slopes_ref, wave_ref, sem):
    copies = [
        pltpu.make_async_copy(wave_in, wave_ref, sem.at[0]),
        pltpu.make_async_copy(slopes_in, slopes_ref, sem.at[1]),
    ]
    for copy in copies:
        copy.start()
    for copy in copies:
        copy.wait()


def local(fields, phases, residual, led_index):
    consts = [jnp.asarray(t) for t in tables()]
    scratch = [
        pltpu.SMEM(led_index.shape, jnp.int32),
        pltpu.VMEM(fields.shape, F32),
        pltpu.VMEM(phases.shape, F32),
    ]
    scratch += [pltpu.VMEM(t.shape, t.dtype) for t in consts]
    scratch += [pltpu.VMEM((2,) + t.shape, BF16) for t in consts[:3]]
    scratch += [
        pltpu.VMEM((HALVES, 2, 2 * PEERS, LANES), F32),
        pltpu.VMEM((SLICES, 2, ROWS, N), F32),
    ]
    to_col = pltpu.VMEM((SLICES, HALVES, LEDS, OWNERS, PART, LANES), F32)
    to_row = pltpu.VMEM((SLICES, HALVES, PEERS, PART, LANES), F32)
    scratch += [to_col, to_row, to_row, to_col]
    scratch += [
        pltpu.VMEM((SLICES, GROUPS, ROWS, LANES), F32),
        pltpu.VMEM((SLICES, GROUPS, ROWS, LANES), F32),
        pltpu.SemaphoreType.DMA((9,)),
        pltpu.SemaphoreType.DMA((SLICES, HALVES)),
        pltpu.SemaphoreType.DMA((SLICES, HALVES)),
        pltpu.SemaphoreType.DMA((SLICES, HALVES)),
        pltpu.SemaphoreType.DMA((SLICES, HALVES, LEDS)),
        pltpu.SemaphoreType.DMA((SLICES,)),
        pltpu.SemaphoreType.DMA((SLICES,)),
    ]
    held = [
        pltpu.with_memory_space_constraint(x, pltpu.HBM) for x in [led_index, fields, phases, residual] + consts
    ]
    anywhere = pl.BlockSpec(memory_space=pl.ANY)
    results = pl.pallas_call(
        kernel,
        out_shape=(
            pltpu.VMEM((SLICES, ROWS, LANES), F32),
            pltpu.VMEM(residual.shape, F32),
        ),
        in_specs=[anywhere] * 9,
        out_specs=(pl.BlockSpec(memory_space=pltpu.VMEM),) * 2,
        scratch_shapes=scratch,
        compiler_params=pltpu.CompilerParams(
            collective_id=0, has_side_effects=True, vmem_limit_bytes=VMEM_LIMIT
        ),
        name="adjoint",
    )(*held)
    return pl.pallas_call(
        emit_kernel,
        out_shape=(
            pltpu.HBM((SLICES, ROWS, LANES), F32),
            pltpu.HBM(residual.shape, F32),
        ),
        in_specs=[anywhere] * 2,
        out_specs=(anywhere, anywhere),
        scratch_shapes=[pltpu.SemaphoreType.DMA((2,))],
        name="emit",
    )(*[pltpu.with_memory_space_constraint(x, pltpu.VMEM) for x in results])


def solution(mesh):
    in_specs = (
        P(None, "led", None, "row", None),
        P(None, "row", None),
        P("led", None, "row", None),
        P("led"),
    )
    out_specs = (P(None, "row", "led"), P("led", None, "row", None))
    return jax.shard_map(local, mesh=mesh, in_specs=in_specs, out_specs=out_specs, check_vma=False)
```
